512 devices in a mesh: gx: 16 (over x, z_lo), gy: 8 (over z_hi, core), gz: 4 (over y).
Axes of the slice: x: 4, y: 4, z: 16 (z_hi: 4, z_lo: 4; z = z_hi * 4 + z_lo), core: 2. Of those that a mesh axis runs over, the one named last changes fastest.
Arguments:
- offsets: float32 [3, 32, 16, 8, 128], P(None, 'gx', 'gy', 'gz'), may hold values from 0 to 1
- velocities: float32 [3, 32, 16, 8, 128], P(None, 'gx', 'gy', 'gz'), may hold values from -3 to 3
- smoothing: float32 [32, 16, 8, 128], P('gx', 'gy', 'gz'), may hold values from 0.6 to 1
- mass: float32 [32, 16, 8, 128], P('gx', 'gy', 'gz'), may hold values from 0.004 to 0.016
- entropy: float32 [32, 16, 8, 128], P('gx', 'gy', 'gz'), may hold values from 0.5 to 2
- prior_density: float32 [32, 16, 8, 128], P('gx', 'gy', 'gz'), may hold values from 0.5 to 2
- active: int32 [32, 16, 8, 128], P('gx', 'gy', 'gz'), may hold values from 0 to 1, as said below
Outputs:
- density: float32 [32, 16, 8, 128], P('gx', 'gy', 'gz')
- acceleration: float32 [3, 32, 16, 8, 128], P(None, 'gx', 'gy', 'gz')
The draws below stay inside these ranges and needn't reach their ends.
Inputs may be any that keep to these rules, and one draw needn't show every extreme that they name: 1 marks an active particle; activity is set in aligned blocks of 2 x 2 x 2 cells, and some blocks hold no active particle.
All inputs are finite; a program needn't handle non-finite values.
Results may differ from the reference program's by a relative error of at most 0.0001.
Values sent between devices are 32-bit elements; how exact they have to be, the bound alone decides.
A program may use at most 64 MiB of HBM per device.

```python
import math
import jax
import jax.numpy as jnp
from jax import lax

P_SIZE = 128
NX = 32
NY = 16
NZ = 8


def draw_active(key, part):
    level_key, bit_key = jax.random.split(jax.random.fold_in(key, 11))
    levels = jax.random.randint(level_key, (NX // 2, NY // 2, NZ // 2), 0, 4)
    table = jnp.array([0, 0, 6, 26], dtype=jnp.int32)
    cutoff = table[levels]
    cutoff = jnp.repeat(jnp.repeat(jnp.repeat(cutoff, 2, axis=0), 2, axis=1), 2, axis=2)
    draws = jax.random.randint(bit_key, (NX, NY, NZ, P_SIZE), 0, 64)
    return (draws < cutoff[..., None]).astype(jnp.int32)


def block_levels(key, extent, pieces, smallest, high):
    level = 1.0
    for dim, blocks in pieces:
        steps = jax.random.uniform(jax.random.fold_in(jax.random.fold_in(key, 6), dim), (blocks,), jnp.float32, smallest / len(pieces), high / len(pieces))
        level = level * jnp.repeat(jnp.exp(steps), extent[dim] // blocks).reshape((-1,) + (1,) * (len(extent) - 1 - dim))
    return level


def scatter_about(stream_key, extent, spread, bound, cuts=(), kind=jnp.bfloat16):
    drawn = jax.random.normal(stream_key, extent, jnp.float32) * spread
    if len(cuts) > 0:
        drawn = block_levels(stream_key, extent, cuts, -0.22, 0.18) * drawn
    return jnp.clip(drawn, min=-bound, max=bound).astype(kind)


def setup_inputs(seed: int = 0) -> dict:
    seeds = jax.random.split(jax.random.key(seed), 8)
    offsets = jnp.clip(1.0 * jax.random.uniform(seeds[0], (3, NX, NY, NZ, P_SIZE), jnp.float32) ** block_levels(seeds[0], (3, NX, NY, NZ, P_SIZE), ((1, 16), (2, 8), (3, 4)), -0.2, 0.2), 0.0, 1.0)
    velocities = scatter_about(seeds[1], (3, NX, NY, NZ, P_SIZE), 0.5, 3.0, ((1, 16), (2, 8), (3, 4)), jnp.float32)
    smoothing = jnp.clip(jnp.exp(math.log(1.0) - 0.5108256 * jax.random.uniform(seeds[2], (NX, NY, NZ, P_SIZE), jnp.float32) ** block_levels(seeds[2], (NX, NY, NZ, P_SIZE), ((0, 16), (1, 8), (2, 4)), -0.2, 0.2)), 0.6, 1.0)
    mass = jnp.clip(jnp.exp(math.log(0.016) - 1.3862944 * jax.random.uniform(seeds[3], (NX, NY, NZ, P_SIZE), jnp.float32) ** block_levels(seeds[3], (NX, NY, NZ, P_SIZE), ((0, 16), (1, 8), (2, 4)), -0.2, 0.2)), 0.004, 0.016)
    entropy = jnp.clip(jnp.exp(math.log(2.0) - 1.3862944 * jax.random.uniform(seeds[4], (NX, NY, NZ, P_SIZE), jnp.float32) ** block_levels(seeds[4], (NX, NY, NZ, P_SIZE), ((0, 16), (1, 8), (2, 4)), -0.2, 0.2)), 0.5, 2.0)
    prior_density = jnp.clip(jnp.exp(math.log(2.0) - 1.3862944 * jax.random.uniform(seeds[5], (NX, NY, NZ, P_SIZE), jnp.float32) ** block_levels(seeds[5], (NX, NY, NZ, P_SIZE), ((0, 16), (1, 8), (2, 4)), -0.2, 0.2)), 0.5, 2.0)
    active = draw_active(jax.random.fold_in(seeds[7], 71), 0)
    return {"offsets": offsets, "velocities": velocities, "smoothing": smoothing, "mass": mass, "entropy": entropy, "prior_density": prior_density, "active": active}


kernel_norm = 21.0 / (2.0 * math.pi)
visc_alpha = 1.0
visc_beta = 2.0

def neighbour_shifts():
    return [(step_x, step_y, step_z) for step_x in (-1, 0, 1) for step_y in (-1, 0, 1) for step_z in (-1, 0, 1)]

def kernel_terms(radius_sq, smooth):
    ratio = jnp.sqrt(radius_sq) / smooth
    inside = jnp.maximum(1.0 - ratio, 0.0)
    value = kernel_norm / smooth ** 3 * inside ** 4 * (1.0 + 4.0 * ratio)
    slope = -20.0 * kernel_norm / smooth ** 5 * inside ** 3
    return (value, slope)

def neighbour_cells(around, shift, center):
    size_x, size_y, size_z = (center.shape[1], center.shape[2], center.shape[3])
    return around[:, 1 + shift[0]:1 + shift[0] + size_x, 1 + shift[1]:1 + shift[1] + size_y, 1 + shift[2]:1 + shift[2] + size_z]

def separation(center, neighbour, shift):
    return [center[axis_id][..., :, None] - neighbour[axis_id][..., None, :] - float(shift[axis_id]) for axis_id in range(3)]

def density_block(around):
    center = around[:, 1:-1, 1:-1, 1:-1]
    smooth = center[6][..., :, None]
    total = jnp.zeros(center.shape[1:], jnp.float32)
    for shift in neighbour_shifts():
        neighbour = neighbour_cells(around, shift, center)
        parts = separation(center, neighbour, shift)
        radius_sq = parts[0] ** 2 + parts[1] ** 2 + parts[2] ** 2
        value, slope = kernel_terms(radius_sq, smooth)
        total = total + lax.optimization_barrier(jnp.sum(neighbour[7][..., None, :] * value, axis=-1))
    return total

def force_block(around):
    center = around[:, 1:-1, 1:-1, 1:-1]
    smooth_own = center[6][..., :, None]
    dens_own = center[8][..., :, None]
    factor_own = center[9][..., :, None]
    sound_own = center[10][..., :, None]
    totals = [jnp.zeros(center.shape[1:], jnp.float32) for axis_id in range(3)]
    for shift in neighbour_shifts():
        neighbour = neighbour_cells(around, shift, center)
        parts = separation(center, neighbour, shift)
        radius_sq = parts[0] ** 2 + parts[1] ** 2 + parts[2] ** 2
        approach = parts[0] * (center[3][..., :, None] - neighbour[3][..., None, :])
        approach = approach + parts[1] * (center[4][..., :, None] - neighbour[4][..., None, :])
        approach = approach + parts[2] * (center[5][..., :, None] - neighbour[5][..., None, :])
        smooth_far = neighbour[6][..., None, :]
        value_own, slope_own = kernel_terms(radius_sq, smooth_own)
        value_far, slope_far = kernel_terms(radius_sq, smooth_far)
        mean_smooth = 0.5 * (smooth_own + smooth_far)
        closing = mean_smooth * jnp.minimum(approach, 0.0) / (radius_sq + 0.01 * mean_smooth ** 2)
        viscous = (-visc_alpha * 0.5 * (sound_own + neighbour[10][..., None, :]) * closing + visc_beta * closing ** 2) / (0.5 * (dens_own + neighbour[8][..., None, :]))
        weight = neighbour[7][..., None, :] * (factor_own * slope_own + neighbour[9][..., None, :] * slope_far + viscous * 0.5 * (slope_own + slope_far))
        for axis_id in range(3):
            totals[axis_id] = totals[axis_id] - lax.optimization_barrier(jnp.sum(weight * parts[axis_id], axis=-1))
    return jnp.stack(totals)

def reference(offsets, velocities, smoothing, mass, entropy, prior_density, active):
    fields = jnp.concatenate([offsets, velocities, smoothing[None], mass[None], entropy[None]], axis=0)
    pad_width = ((0, 0), (1, 1), (1, 1), (1, 1), (0, 0))
    padded = jnp.pad(fields, pad_width, mode='wrap')

    def density_slab(index):
        return density_block(lax.dynamic_slice_in_dim(padded, index, 3, 1))[0]
    computed = lax.map(density_slab, jnp.arange(NX, dtype=jnp.int32))
    live = active == 1
    density = jnp.where(live, computed, prior_density)
    factor = entropy * density ** (-1.0 / 3.0)
    sound = jnp.sqrt(5.0 / 3.0 * entropy * density ** (2.0 / 3.0))
    forces = jnp.concatenate([fields[:8], density[None], factor[None], sound[None]], axis=0)
    padded_force = jnp.pad(forces, pad_width, mode='wrap')

    def force_slab(index):
        return force_block(lax.dynamic_slice_in_dim(padded_force, index, 3, 1))[:, 0]
    accel = jnp.moveaxis(lax.map(force_slab, jnp.arange(NX, dtype=jnp.int32)), 0, 1)
    accel = jnp.where(live[None], accel, 0.0)
    return (density, accel)
```

```python
import functools
import math

import jax
import jax.numpy as jnp
from jax import lax
from jax.experimental import pallas as pl
from jax.experimental.pallas import tpu as pltpu
from jax.sharding import PartitionSpec as P

MESH = pl.DeviceIdType.MESH
AXES = ("gx", "gy", "gz")
KERNEL_NORM = 21.0 / (2.0 * math.pi)
F32 = jnp.float32
LANES = 128
VMEM_BYTES = 24 * 1024 * 1024

AROUND = sorted(
    (
        (a, b, c)
        for a in (-1, 0, 1)
        for b in (-1, 0, 1)
        for c in (-1, 0, 1)
        if (a, b, c) != (0, 0, 0)
    ),
    key=lambda d: (-abs(d[1]), -abs(d[0]), -abs(d[2]), d),
)
STEPS = [16 * a + 4 * b + c for a in (-1, 0, 1) for b in (-1, 0, 1) for c in (-1, 0, 1)]


def device_at(step, sizes):
    return tuple(
        lax.rem(lax.axis_index(axis) + (move + size), size) if move else lax.axis_index(axis)
        for axis, move, size in zip(AXES, step, sizes)
    )


def leaving(step):
    return tuple({0: pl.ds(1, 2), 1: pl.ds(2, 1), -1: pl.ds(1, 1)}[move] for move in step)


def arriving(step):
    return tuple({0: pl.ds(1, 2), 1: pl.ds(0, 1), -1: pl.ds(3, 1)}[move] for move in step)


def greet(sizes):
    barrier = pltpu.get_barrier_semaphore()
    for step in AROUND:
        pl.semaphore_signal(
            barrier, inc=1, device_id=device_at(step, sizes), device_id_type=MESH
        )


def exchange(cells, sizes, send_sem, recv_sem):
    pl.semaphore_wait(pltpu.get_barrier_semaphore(), len(AROUND))
    copies = []
    for index, step in enumerate(AROUND):
        copy = pltpu.make_async_remote_copy(
            src_ref=cells.at[leaving(step)],
            dst_ref=cells.at[arriving(step)],
            send_sem=send_sem.at[index],
            recv_sem=recv_sem.at[index],
            device_id=device_at(step, sizes),
            device_id_type=MESH,
        )
        copy.start()
        copies.append(copy)
    for copy in copies:
        copy.wait()


def fields_kernel(sizes, offsets, velocities, smoothing, mass, cells, send_sem, recv_sem):
    greet(sizes)
    for c in range(8):
        x, y, z = 1 + c // 4, 1 + (c // 2) % 2, 1 + c % 2
        rows = [offsets[8 * d + c : 8 * d + c + 1] for d in range(3)]
        rows += [mass[c : c + 1]]
        rows += [velocities[8 * d + c : 8 * d + c + 1] for d in range(3)]
        rows += [smoothing[c : c + 1]]
        for row, value in enumerate(rows):
            cells[x, y, z, row : row + 1, :] = value
    exchange(cells, sizes, send_sem, recv_sem)


def density_exchange_kernel(sizes, density, factor, cells, send_sem, recv_sem):
    greet(sizes)
    for c in range(8):
        x, y, z = 1 + c // 4, 1 + (c // 2) % 2, 1 + c % 2
        cells[x, y, z, 0:1, :] = density[c : c + 1]
        cells[x, y, z, 1:2, :] = factor[c : c + 1]
    exchange(cells, sizes, send_sem, recv_sem)


def wide(row):
    return jnp.broadcast_to(row, (8, LANES))


def corner(c):
    return (
        lax.convert_element_type(c // 16, F32),
        lax.convert_element_type((c // 4) % 4, F32),
        lax.convert_element_type(c % 4, F32),
    )


def own_cell(c):
    return 16 * (1 + c // 4) + 4 * (1 + (c // 2) % 2) + 1 + c % 2


def rank_active(active, ranks, counts):
    live = active[...] == 1
    flags = jnp.where(live, 1.0, 0.0).astype(F32)
    ahead = lax.broadcasted_iota(jnp.int32, (LANES, LANES), 0) < lax.broadcasted_iota(
        jnp.int32, (LANES, LANES), 1
    )
    before = jnp.dot(
        flags.astype(jnp.bfloat16),
        jnp.where(ahead, 1.0, 0.0).astype(jnp.bfloat16),
        preferred_element_type=F32,
    )
    ranks[...] = jnp.where(live, before, -1.0)
    for c in range(8):
        counts[c] = jnp.sum(flags[c : c + 1]).astype(jnp.int32)


def chosen(ranks, c, group):
    places = lax.broadcasted_iota(jnp.int32, (8, LANES), 0) + 8 * group
    return wide(ranks[pl.ds(c, 1), :]) == places.astype(F32)


def pick(mask, row):
    return jnp.sum(jnp.where(mask, row, 0.0), axis=1, keepdims=True)


def density_kernel(cells, active, entropy, prior, density, factor, spread, ranks, counts):
    rank_active(active, ranks, counts)

    def prepare(c, carry):
        px, py, pz = corner(c)
        spread[4 * c] = wide(4.0 * (cells[c, 0:1, :] + px))
        spread[4 * c + 1] = wide(4.0 * (cells[c, 1:2, :] + py))
        spread[4 * c + 2] = wide(4.0 * (cells[c, 2:3, :] + pz))
        spread[4 * c + 3] = wide(cells[c, 3:4, :])
        return carry

    lax.fori_loop(0, 64, prepare, 0, unroll=4)

    def cell(c, carry):
        here = own_cell(c)

        def group_step(group, total):
            mask = chosen(ranks, c, group)
            xi = wide_lanes(pick(mask, spread[4 * here]))
            yi = wide_lanes(pick(mask, spread[4 * here + 1]))
            zi = wide_lanes(pick(mask, spread[4 * here + 2]))
            hi = wide_lanes(pick(mask, wide(cells[here, 7:8, :])))
            hi4 = 4.0 * hi
            acc = jnp.zeros((8, LANES), F32)
            for step in STEPS:
                j = 4 * (here + step)
                dx = xi - spread[j]
                dy = yi - spread[j + 1]
                dz = zi - spread[j + 2]
                sq = dx * dx + dy * dy + dz * dz
                r4 = sq * lax.rsqrt(jnp.maximum(sq, 1e-30))
                u = jnp.maximum(hi4 - r4, 0.0)
                u2 = u * u
                acc = acc + (u2 * u2) * ((hi + r4) * spread[j + 3])
            h2 = hi * hi
            h4 = h2 * h2
            value = jnp.sum(acc, axis=1, keepdims=True) * ((KERNEL_NORM / 256.0) / (h4 * h4))
            return total + jnp.where(mask, value, 0.0)

        total = lax.fori_loop(
            0, (counts[c] + 7) // 8, group_step, jnp.zeros((8, LANES), F32)
        )
        density[pl.ds(c, 1), :] = jnp.sum(total, axis=0, keepdims=True)
        return carry

    lax.fori_loop(0, 8, cell, 0)
    value = jnp.where(active[...] == 1, density[...], prior[...])
    density[...] = value
    factor[...] = entropy[...] * jnp.exp(jnp.log(value) * (-1.0 / 3.0))


def wide_lanes(column):
    return jnp.broadcast_to(column, (8, LANES))


FIELDS = 13


def strength(h):
    h2 = h * h
    h4 = h2 * h2
    return (2.5 * KERNEL_NORM) / (h4 * h4)


def force_kernel(cells, states, active, accel, spread, ranks, counts):
    rank_active(active, ranks, counts)

    def prepare(c, carry):
        px, py, pz = corner(c)
        at = FIELDS * c
        tile = cells[c]
        mass, h = tile[3:4], tile[7:8]
        rho = states[c, 0:1, :]
        fac = states[c, 1:2, :]
        rows = [tile[0:1] + px, tile[1:2] + py, tile[2:3] + pz]
        rows += [40.0 * tile[4:5], 40.0 * tile[5:6], 40.0 * tile[6:7]]
        rows += [h, 0.05 * h, mass * strength(h), mass]
        rows += [rho, 8.0 * fac, jnp.sqrt((5.0 / 3.0) * fac * rho)]
        for k, row in enumerate(rows):
            spread[at + k] = wide(row)
        return carry

    lax.fori_loop(0, 64, prepare, 0, unroll=2)

    def cell(c, carry):
        here = own_cell(c)

        def group_step(group, totals):
            mask = chosen(ranks, c, group)
            own = [
                wide_lanes(pick(mask, spread[FIELDS * here + k]))
                for k in (0, 1, 2, 3, 4, 5, 6, 7, 10, 11, 12)
            ]
            xi, yi, zi, ui_x, ui_y, ui_z, hi, ei, rhoi, faci, soundi = own
            bi = strength(hi)
            ax = jnp.zeros((8, LANES), F32)
            ay = jnp.zeros((8, LANES), F32)
            az = jnp.zeros((8, LANES), F32)
            for step in STEPS:
                j = FIELDS * (here + step)
                dx = xi - spread[j]
                dy = yi - spread[j + 1]
                dz = zi - spread[j + 2]
                sq = dx * dx + dy * dy + dz * dz
                app = (
                    dx * (ui_x - spread[j + 3])
                    + dy * (ui_y - spread[j + 4])
                    + dz * (ui_z - spread[j + 5])
                )
                r = sq * lax.rsqrt(jnp.maximum(sq, 1e-30))
                near = jnp.maximum(hi - r, 0.0)
                far = jnp.maximum(spread[j + 6] - r, 0.0)
                e = ei + spread[j + 7]
                m = e * jnp.minimum(app, 0.0) / (sq + e * e)
                visc = m * (m - (soundi + spread[j + 12])) / (rhoi + spread[j + 10])
                g_near = (near * near) * (near * (bi * spread[j + 9]))
                g_far = (far * far) * (far * spread[j + 8])
                w = (faci + visc) * g_near + (spread[j + 11] + visc) * g_far
                ax = ax + w * dx
                ay = ay + w * dy
                az = az + w * dz
            return tuple(
                total + jnp.where(mask, jnp.sum(a, axis=1, keepdims=True), 0.0)
                for total, a in zip(totals, (ax, ay, az))
            )

        zero = jnp.zeros((8, LANES), F32)
        totals = lax.fori_loop(0, (counts[c] + 7) // 8, group_step, (zero, zero, zero))
        for d in range(3):
            accel[pl.ds(8 * d + c, 1), :] = jnp.sum(totals[d], axis=0, keepdims=True)
        return carry

    lax.fori_loop(0, 8, cell, 0)


def vmem(count):
    return [pl.BlockSpec(memory_space=pltpu.VMEM)] * count


def remote_call(kernel, rows, count, collective_id):
    return pl.pallas_call(
        kernel,
        out_shape=jax.ShapeDtypeStruct((4, 4, 4, rows, LANES), F32),
        in_specs=vmem(count),
        out_specs=vmem(1)[0],
        scratch_shapes=[
            pltpu.SemaphoreType.DMA((len(AROUND),)),
            pltpu.SemaphoreType.DMA((len(AROUND),)),
        ],
        compiler_params=pltpu.CompilerParams(
            collective_id=collective_id, has_side_effects=True, vmem_limit_bytes=VMEM_BYTES
        ),
    )


def body(sizes, offsets, velocities, smoothing, mass, entropy, prior_density, active):
    flat = lambda a: a.reshape(-1, LANES)
    offsets, velocities = flat(offsets), flat(velocities)
    smoothing, mass, entropy = flat(smoothing), flat(mass), flat(entropy)
    prior_density, active = flat(prior_density), flat(active)
    cells = remote_call(functools.partial(fields_kernel, sizes), 8, 4, 0)(
        offsets, velocities, smoothing, mass
    ).reshape(64, 8, LANES)
    own = jax.ShapeDtypeStruct((8, LANES), F32)
    density, factor = pl.pallas_call(
        density_kernel,
        out_shape=(own, own),
        in_specs=vmem(4),
        out_specs=tuple(vmem(2)),
        scratch_shapes=[
            pltpu.VMEM((4 * 64, 8, LANES), F32),
            pltpu.VMEM((8, LANES), F32),
            pltpu.SMEM((8,), jnp.int32),
        ],
        compiler_params=pltpu.CompilerParams(vmem_limit_bytes=VMEM_BYTES),
    )(cells, active, entropy, prior_density)
    states = remote_call(functools.partial(density_exchange_kernel, sizes), 2, 2, 1)(
        density, factor
    ).reshape(64, 2, LANES)
    accel = pl.pallas_call(
        force_kernel,
        out_shape=jax.ShapeDtypeStruct((24, LANES), F32),
        in_specs=vmem(3),
        out_specs=vmem(1)[0],
        scratch_shapes=[
            pltpu.VMEM((FIELDS * 64, 8, LANES), F32),
            pltpu.VMEM((8, LANES), F32),
            pltpu.SMEM((8,), jnp.int32),
        ],
        compiler_params=pltpu.CompilerParams(vmem_limit_bytes=VMEM_BYTES),
    )(cells, states, active)
    return density.reshape(2, 2, 2, LANES), accel.reshape(3, 2, 2, 2, LANES)


def solution(mesh):
    sizes = tuple(mesh.shape[axis] for axis in AXES)
    spec = P("gx", "gy", "gz", None)
    spec3 = P(None, "gx", "gy", "gz", None)
    return jax.shard_map(
        functools.partial(body, sizes),
        mesh=mesh,
        in_specs=(spec3, spec3, spec, spec, spec, spec, spec),
        out_specs=(spec, spec3),
        check_vma=False,
    )
```

```python
import functools
import math

import jax
import jax.numpy as jnp
from jax import lax
from jax.experimental import pallas as pl
from jax.experimental.pallas import tpu as pltpu
from jax.sharding import PartitionSpec as P

MESH = pl.DeviceIdType.MESH
AXES = ("gx", "gy", "gz")
KERNEL_NORM = 21.0 / (2.0 * math.pi)
F32 = jnp.float32
LANES = 128
VMEM_BYTES = 30 * 1024 * 1024

AROUND = sorted(
    (
        (a, b, c)
        for a in (-1, 0, 1)
        for b in (-1, 0, 1)
        for c in (-1, 0, 1)
        if (a, b, c) != (0, 0, 0)
    ),
    key=lambda d: (-abs(d[1]), -abs(d[0]), -abs(d[2]), d),
)
COUNT = len(AROUND)
JX, JY, JZ, JM, JU, JV, JW, JH, JE, JB = range(10)
J_TILES = 10
JR, JF, JS = range(3)
S_TILES = 3
IX, IY, IZ, IH, IU, IV, IW, IE, IB, IR, IF, IS = range(12)
I_TILES = 12
GROUPS = 16
OWN = [(x, y, z) for x in (1, 2) for y in (1, 2) for z in (1, 2)]
GHOST = [
    (x, y, z)
    for x in range(4)
    for y in range(4)
    for z in range(4)
    if not (x in (1, 2) and y in (1, 2) and z in (1, 2))
]


def device_at(step, sizes):
    return tuple(
        lax.rem(lax.axis_index(axis) + (move + size), size) if move else lax.axis_index(axis)
        for axis, move, size in zip(AXES, step, sizes)
    )


def leaving(step):
    return tuple({0: pl.ds(1, 2), 1: pl.ds(2, 1), -1: pl.ds(1, 1)}[move] for move in step)


def arriving(step):
    return tuple({0: pl.ds(1, 2), 1: pl.ds(0, 1), -1: pl.ds(3, 1)}[move] for move in step)


def send_all(cells, sizes, send_sem, recv_sem):
    copies = {}
    for index, step in enumerate(AROUND):
        copies[step] = pltpu.make_async_remote_copy(
            src_ref=cells.at[leaving(step)],
            dst_ref=cells.at[arriving(step)],
            send_sem=send_sem.at[index],
            recv_sem=recv_sem.at[index],
            device_id=device_at(step, sizes),
            device_id_type=MESH,
        )
        copies[step].start()
    return copies


def flat(x, y, z):
    return 16 * x + 4 * y + z


def wide(row):
    return jnp.broadcast_to(row, (8, LANES))


def strength(h4):
    h2 = h4 * h4
    q = h2 * h2
    return (2.5 * KERNEL_NORM * 1024.0) / (q * q)


def ranks_of(active, order):
    live = active == 1
    before = jnp.dot(
        jnp.where(live, 1.0, 0.0).astype(jnp.bfloat16),
        order.astype(jnp.bfloat16),
        preferred_element_type=F32,
    )
    return jnp.where(live, before, -1.0)


def order_kernel(order):
    ahead = lax.broadcasted_iota(jnp.int32, (LANES, LANES), 0) < lax.broadcasted_iota(
        jnp.int32, (LANES, LANES), 1
    )
    order[...] = jnp.where(ahead, 1.0, 0.0)


def chosen(ranks, c, group):
    places = lax.broadcasted_iota(jnp.int32, (8, LANES), 0) + 8 * group
    return wide(ranks[pl.ds(c, 1), :]) == places.astype(F32)


def across(tile):
    return jnp.broadcast_to(jnp.sum(tile, axis=1, keepdims=True), (8, LANES))


def density_sum(own, spread, sites, acc):
    x, y, z, h4 = own
    h = 0.25 * h4
    for site in sites:
        j = J_TILES * site
        dx = x - spread[j + JX]
        dy = y - spread[j + JY]
        dz = z - spread[j + JZ]
        sq = dx * dx + dy * dy + dz * dz
        r4 = sq * lax.rsqrt(jnp.maximum(sq, 1e-30))
        u = jnp.maximum(h4 - r4, 0.0)
        u2 = u * u
        acc = acc + (u2 * u2) * ((h + r4) * spread[j + JM])
    return acc


def force_sum(own, spread, states, sites, acc):
    x, y, z, h4, vx, vy, vz, e4, b, rho, fac, sound = own
    ax, ay, az = acc
    for site in sites:
        j = J_TILES * site
        s = S_TILES * site
        dx = x - spread[j + JX]
        dy = y - spread[j + JY]
        dz = z - spread[j + JZ]
        sq = dx * dx + dy * dy + dz * dz
        app = dx * (vx - spread[j + JU]) + dy * (vy - spread[j + JV]) + dz * (vz - spread[j + JW])
        r4 = sq * lax.rsqrt(jnp.maximum(sq, 1e-30))
        near = jnp.maximum(h4 - r4, 0.0)
        far = jnp.maximum(spread[j + JH] - r4, 0.0)
        e = e4 + spread[j + JE]
        m = e * jnp.minimum(app, 0.0) / (sq + e * e)
        visc = m * (m - (sound + states[s + JS])) / (rho + states[s + JR])
        g_near = (near * near) * (near * (b * spread[j + JM]))
        g_far = (far * far) * (far * spread[j + JB])
        w = (fac + visc) * g_near + (states[s + JF] + visc) * g_far
        ax = ax + w * dx
        ay = ay + w * dy
        az = az + w * dz
    return ax, ay, az


def ghost_sites(c, which):
    gx, gy, gz = 3 * (c // 4), 3 * ((c // 2) % 2), 3 * (c % 2)
    z_side = [flat(x, y, gz) for x in (1, 2) for y in (1, 2)]
    x_side = [flat(gx, y, z) for y in (1, 2) for z in (1, 2, gz)]
    y_side = [flat(x, gy, z) for x in (1, 2, gx) for z in (1, 2, gz)]
    return {"z": z_side, "x": x_side, "y": y_side}[which]


def own_sites():
    return [flat(x, y, z) for x, y, z in OWN]


def place_tiles(cells, spread, x, y, z):
    at = J_TILES * flat(x, y, z)
    spread[at + JX] = wide(4.0 * (cells[x, y, z, 0:1, :] + float(x)))
    spread[at + JY] = wide(4.0 * (cells[x, y, z, 1:2, :] + float(y)))
    spread[at + JZ] = wide(4.0 * (cells[x, y, z, 2:3, :] + float(z)))
    spread[at + JM] = wide(cells[x, y, z, 3:4, :])


def motion_tiles(cells, spread, x, y, z):
    at = J_TILES * flat(x, y, z)
    tile = cells[x, y, z]
    h4 = 4.0 * tile[7:8]
    spread[at + JU] = wide(40.0 * tile[4:5])
    spread[at + JV] = wide(40.0 * tile[5:6])
    spread[at + JW] = wide(40.0 * tile[6:7])
    spread[at + JH] = wide(h4)
    spread[at + JE] = wide(0.05 * h4)
    spread[at + JB] = wide(tile[3:4] * strength(h4))


def state_tiles(rho, fac, states, site):
    at = S_TILES * site
    states[at + JR] = wide(rho)
    states[at + JF] = wide(8.0 * fac)
    states[at + JS] = wide(jnp.sqrt((5.0 / 3.0) * fac * rho))


def gather_kernel(
    sizes,
    order,
    offsets,
    velocities,
    smoothing,
    mass,
    entropy,
    prior,
    active,
    spread,
    particles,
    partial,
    gas,
    ranks,
    density,
    cells,
    own_states,
    sums,
    send_sem,
    recv_sem,
    send2_sem,
    recv2_sem,
):
    barrier = pltpu.get_barrier_semaphore()
    for step in AROUND:
        pl.semaphore_signal(
            barrier, inc=1, device_id=device_at(step, sizes), device_id_type=MESH
        )
    for c, (x, y, z) in enumerate(OWN):
        rows = [offsets[8 * d + c : 8 * d + c + 1] for d in range(3)]
        rows += [mass[c : c + 1]]
        rows += [velocities[8 * d + c : 8 * d + c + 1] for d in range(3)]
        rows += [smoothing[c : c + 1]]
        for row, value in enumerate(rows):
            cells[x, y, z, row : row + 1, :] = value
    pl.semaphore_wait(barrier, COUNT)
    copies = send_all(cells, sizes, send_sem, recv_sem)

    for x, y, z in OWN:
        place_tiles(cells, spread, x, y, z)
        motion_tiles(cells, spread, x, y, z)
    ranks[...] = ranks_of(active[...], order[...])

    def pick(t, carry):
        c, group = t // GROUPS, t % GROUPS
        here = J_TILES * flat(1 + c // 4, 1 + (c // 2) % 2, 1 + c % 2)
        mask = chosen(ranks, c, group)
        at = I_TILES * t
        for i_tile, j_tile in (
            (IX, JX),
            (IY, JY),
            (IZ, JZ),
            (IU, JU),
            (IV, JV),
            (IW, JW),
        ):
            particles[at + i_tile] = across(jnp.where(mask, spread[here + j_tile], 0.0))
        h4 = across(jnp.where(mask, spread[here + JH], 0.0))
        particles[at + IH] = h4
        particles[at + IE] = 0.05 * h4
        particles[at + IB] = strength(h4)
        particles[at + IF] = across(jnp.where(mask, wide(entropy[pl.ds(c, 1), :]), 0.0))
        return carry

    lax.fori_loop(0, 8 * GROUPS, pick, 0, unroll=2)

    def density_inputs(t):
        at = I_TILES * t
        return [particles[at + k] for k in (IX, IY, IZ, IH)]

    def inner_density(t, carry):
        sums[t] = density_sum(
            density_inputs(t), spread, own_sites(), jnp.zeros((8, LANES), F32)
        )
        return carry

    lax.fori_loop(0, 8 * GROUPS, inner_density, 0, unroll=2)

    for which in ("z", "x", "y"):
        axis = {"z": 2, "x": 0, "y": 1}[which]
        later = {"z": (0, 1), "x": (1,), "y": ()}[which]
        for step in AROUND:
            if step[axis] and not any(step[k] for k in later):
                copies[step].wait_recv()
        for x, y, z in GHOST:
            cell = (x, y, z)
            if cell[axis] in (0, 3) and not any(cell[k] in (0, 3) for k in later):
                place_tiles(cells, spread, x, y, z)

        def outer_density(t, carry, which=which):
            sums[t] = density_sum(
                density_inputs(t), spread, ghost_sites(t // GROUPS, which), sums[t]
            )
            return carry

        lax.fori_loop(0, 8 * GROUPS, outer_density, 0, unroll=2)

    def settle(c, carry):
        total = jnp.zeros((8, LANES), F32)
        for group in range(GROUPS):
            t = GROUPS * c + group
            at = I_TILES * t
            mask = chosen(ranks, c, group)
            h4 = particles[at + IH]
            h2 = h4 * h4
            q = h2 * h2
            rho = across(sums[t]) * ((KERNEL_NORM * 256.0) / (q * q))
            total = total + jnp.where(mask, rho, 0.0)
            fac = particles[at + IF] * jnp.exp(jnp.log(rho) * (-1.0 / 3.0))
            particles[at + IR] = rho
            particles[at + IF] = 8.0 * fac
            particles[at + IS] = jnp.sqrt((5.0 / 3.0) * fac * rho)
        density[pl.ds(c, 1), :] = jnp.sum(total, axis=0, keepdims=True)
        return carry

    lax.fori_loop(0, 8, settle, 0)
    rho = jnp.where(active[...] == 1, density[...], prior[...])
    density[...] = rho
    fac = entropy[...] * jnp.exp(jnp.log(rho) * (-1.0 / 3.0))
    for c, (x, y, z) in enumerate(OWN):
        gas[x, y, z, 0:1, :] = rho[c : c + 1]
        gas[x, y, z, 1:2, :] = fac[c : c + 1]
    copies2 = send_all(gas, sizes, send2_sem, recv2_sem)

    for c, (x, y, z) in enumerate(OWN):
        state_tiles(rho[c : c + 1], fac[c : c + 1], own_states, flat(x, y, z))

    def inner_force(t, carry):
        at = I_TILES * t
        zero = jnp.zeros((8, LANES), F32)
        acc = force_sum(
            [particles[at + k] for k in range(I_TILES)],
            spread,
            own_states,
            own_sites(),
            (zero, zero, zero),
        )
        for d in range(3):
            partial[3 * t + d] = acc[d]
        return carry

    lax.fori_loop(0, 8 * GROUPS, inner_force, 0)
    for x, y, z in GHOST:
        motion_tiles(cells, spread, x, y, z)
    for step in AROUND:
        copies[step].wait_send()
        copies2[step].wait()


def force_kernel(
    spread, particles, partial, gas, ranks, density_in, density, accel, states, sums, counts
):
    density[...] = density_in[...]
    last = jnp.max(ranks[...], axis=1, keepdims=True)
    for c in range(8):
        counts[c] = (jnp.max(last[c : c + 1]) + 1.0).astype(jnp.int32)

    def prepare(site, carry):
        state_tiles(gas[site, 0:1, :], gas[site, 1:2, :], states, site)
        return carry

    lax.fori_loop(0, 64, prepare, 0, unroll=4)

    def cell(c, carry):
        groups = (counts[c] + 7) // 8
        sites = [site for which in ("z", "x", "y") for site in ghost_sites(c, which)]

        def group_step(group, inner):
            t = GROUPS * c + group
            at = I_TILES * t
            acc = force_sum(
                [particles[at + k] for k in range(I_TILES)],
                spread,
                states,
                sites,
                tuple(partial[3 * t + d] for d in range(3)),
            )
            for d in range(3):
                sums[3 * group + d] = acc[d]
            return inner

        lax.fori_loop(0, groups, group_step, 0)

        def fold(quad, totals):
            for k in range(4):
                group = 4 * quad + k
                mask = chosen(ranks, c, group)
                totals = tuple(
                    total + jnp.where(mask, across(sums[3 * group + d]), 0.0)
                    for d, total in enumerate(totals)
                )
            return totals

        zero = jnp.zeros((8, LANES), F32)
        totals = lax.fori_loop(0, (groups + 3) // 4, fold, (zero, zero, zero))
        for d in range(3):
            accel[pl.ds(8 * d + c, 1), :] = 0.25 * jnp.sum(totals[d], axis=0, keepdims=True)
        return carry

    lax.fori_loop(0, 8, cell, 0)


def vmem(count):
    return [pl.BlockSpec(memory_space=pltpu.VMEM)] * count


def tiles(count):
    return jax.ShapeDtypeStruct((count, 8, LANES), F32)


def body(sizes, *args):
    rows = [a.reshape(-1, LANES) for a in args]
    cell_rows = jax.ShapeDtypeStruct((8, LANES), F32)
    order = pl.pallas_call(
        order_kernel,
        out_shape=jax.ShapeDtypeStruct((LANES, LANES), F32),
        out_specs=vmem(1)[0],
        compiler_params=pltpu.CompilerParams(vmem_limit_bytes=VMEM_BYTES),
        cost_estimate=pl.CostEstimate(flops=10_000_000, bytes_accessed=8_000_000, transcendentals=0),
    )()
    spread, particles, partial, gas, ranks, density = pl.pallas_call(
        functools.partial(gather_kernel, sizes),
        out_shape=(
            tiles(64 * J_TILES),
            tiles(8 * GROUPS * I_TILES),
            tiles(8 * GROUPS * 3),
            jax.ShapeDtypeStruct((4, 4, 4, 2, LANES), F32),
            cell_rows,
            cell_rows,
        ),
        in_specs=vmem(8),
        out_specs=tuple(vmem(6)),
        scratch_shapes=[
            pltpu.VMEM((4, 4, 4, 8, LANES), F32),
            pltpu.VMEM((64 * S_TILES, 8, LANES), F32),
            pltpu.VMEM((8 * GROUPS, 8, LANES), F32),
            pltpu.SemaphoreType.DMA((COUNT,)),
            pltpu.SemaphoreType.DMA((COUNT,)),
            pltpu.SemaphoreType.DMA((COUNT,)),
            pltpu.SemaphoreType.DMA((COUNT,)),
        ],
        compiler_params=pltpu.CompilerParams(
            collective_id=0, has_side_effects=True, vmem_limit_bytes=VMEM_BYTES
        ),
    )(order, *rows)
    density, accel = pl.pallas_call(
        force_kernel,
        out_shape=(cell_rows, jax.ShapeDtypeStruct((24, LANES), F32)),
        in_specs=vmem(6),
        out_specs=tuple(vmem(2)),
        scratch_shapes=[
            pltpu.VMEM((64 * S_TILES, 8, LANES), F32),
            pltpu.VMEM((GROUPS * 3, 8, LANES), F32),
            pltpu.SMEM((8,), jnp.int32),
        ],
        compiler_params=pltpu.CompilerParams(vmem_limit_bytes=VMEM_BYTES),
    )(spread, particles, partial, gas.reshape(64, 2, LANES), ranks, density)
    return density.reshape(2, 2, 2, LANES), accel.reshape(3, 2, 2, 2, LANES)


def solution(mesh):
    sizes = tuple(mesh.shape[axis] for axis in AXES)
    spec = P("gx", "gy", "gz", None)
    spec3 = P(None, "gx", "gy", "gz", None)
    return jax.shard_map(
        functools.partial(body, sizes),
        mesh=mesh,
        in_specs=(spec3, spec3, spec, spec, spec, spec, spec),
        out_specs=(spec, spec3),
        check_vma=False,
    )
```

```python
import functools
import math

import jax
import jax.numpy as jnp
from jax import lax
from jax.experimental import pallas as pl
from jax.experimental.pallas import tpu as pltpu
from jax.sharding import PartitionSpec as P

MESH = pl.DeviceIdType.MESH
AXES = ("gx", "gy", "gz")
KERNEL_NORM = 21.0 / (2.0 * math.pi)
F32 = jnp.float32
LANES = 128
VMEM_BYTES = 30 * 1024 * 1024

AROUND = sorted(
    (
        (a, b, c)
        for a in (-1, 0, 1)
        for b in (-1, 0, 1)
        for c in (-1, 0, 1)
        if (a, b, c) != (0, 0, 0)
    ),
    key=lambda d: (-abs(d[1]), -abs(d[0]), -abs(d[2]), d),
)
COUNT = len(AROUND)
JX, JY, JZ, JM, JU, JV, JW, JH, JE, JB = range(10)
J_TILES = 10
JR, JF, JS = range(3)
S_TILES = 3
IX, IY, IZ, IH, IU, IV, IW, IE, IB, IR, IF, IS = range(12)
I_TILES = 12
GROUPS = 16
OWN = [(x, y, z) for x in (1, 2) for y in (1, 2) for z in (1, 2)]
GHOST = [
    (x, y, z)
    for x in range(4)
    for y in range(4)
    for z in range(4)
    if not (x in (1, 2) and y in (1, 2) and z in (1, 2))
]


def device_at(step, sizes):
    return tuple(
        lax.rem(lax.axis_index(axis) + (move + size), size) if move else lax.axis_index(axis)
        for axis, move, size in zip(AXES, step, sizes)
    )


def leaving(step):
    return tuple({0: pl.ds(1, 2), 1: pl.ds(2, 1), -1: pl.ds(1, 1)}[move] for move in step)


def arriving(step):
    return tuple({0: pl.ds(1, 2), 1: pl.ds(0, 1), -1: pl.ds(3, 1)}[move] for move in step)


def send_all(cells, sizes, send_sem, recv_sem):
    copies = {}
    for index, step in enumerate(AROUND):
        copies[step] = pltpu.make_async_remote_copy(
            src_ref=cells.at[leaving(step)],
            dst_ref=cells.at[arriving(step)],
            send_sem=send_sem.at[index],
            recv_sem=recv_sem.at[index],
            device_id=device_at(step, sizes),
            device_id_type=MESH,
        )
        copies[step].start()
    return copies


def flat(x, y, z):
    return 16 * x + 4 * y + z


def wide(row):
    return jnp.broadcast_to(row, (8, LANES))


def strength(h4):
    h2 = h4 * h4
    q = h2 * h2
    return (2.5 * KERNEL_NORM * 1024.0) / (q * q)


def ranks_of(active):
    live = active == 1
    ahead = lax.broadcasted_iota(jnp.int32, (LANES, LANES), 0) < lax.broadcasted_iota(
        jnp.int32, (LANES, LANES), 1
    )
    before = jnp.dot(
        jnp.where(live, 1.0, 0.0).astype(jnp.bfloat16),
        jnp.where(ahead, 1.0, 0.0).astype(jnp.bfloat16),
        preferred_element_type=F32,
    )
    return jnp.where(live, before, -1.0)


def chosen(ranks, c, group):
    places = lax.broadcasted_iota(jnp.int32, (8, LANES), 0) + 8 * group
    return wide(ranks[pl.ds(c, 1), :]) == places.astype(F32)


def across(tile):
    return jnp.broadcast_to(jnp.sum(tile, axis=1, keepdims=True), (8, LANES))


def density_sum(owns, spread, sites, accs):
    accs = list(accs)
    for site in sites:
        j = J_TILES * site
        xj, yj, zj, mj = (spread[j + k] for k in (JX, JY, JZ, JM))
        for k, (x, y, z, h4) in enumerate(owns):
            dx = x - xj
            dy = y - yj
            dz = z - zj
            sq = dx * dx + dy * dy + dz * dz
            r4 = sq * lax.rsqrt(jnp.maximum(sq, 1e-30))
            u = jnp.maximum(h4 - r4, 0.0)
            u2 = u * u
            accs[k] = accs[k] + (u2 * u2) * ((0.25 * h4 + r4) * mj)
    return accs


def force_sum(own, spread, states, sites, acc):
    x, y, z, h4, vx, vy, vz, e4, b, rho, fac, sound = own
    ax, ay, az = acc
    for site in sites:
        j = J_TILES * site
        s = S_TILES * site
        dx = x - spread[j + JX]
        dy = y - spread[j + JY]
        dz = z - spread[j + JZ]
        sq = dx * dx + dy * dy + dz * dz
        app = dx * (vx - spread[j + JU]) + dy * (vy - spread[j + JV]) + dz * (vz - spread[j + JW])
        r4 = sq * lax.rsqrt(jnp.maximum(sq, 1e-30))
        near = jnp.maximum(h4 - r4, 0.0)
        far = jnp.maximum(spread[j + JH] - r4, 0.0)
        e = e4 + spread[j + JE]
        m = e * jnp.minimum(app, 0.0) / (sq + e * e)
        visc = m * (m - (sound + states[s + JS])) / (rho + states[s + JR])
        g_near = (near * near) * (near * (b * spread[j + JM]))
        g_far = (far * far) * (far * spread[j + JB])
        w = (fac + visc) * g_near + (states[s + JF] + visc) * g_far
        ax = ax + w * dx
        ay = ay + w * dy
        az = az + w * dz
    return ax, ay, az


def ghost_sites(c, which):
    gx, gy, gz = 3 * (c // 4), 3 * ((c // 2) % 2), 3 * (c % 2)
    z_side = [flat(x, y, gz) for x in (1, 2) for y in (1, 2)]
    x_side = [flat(gx, y, z) for y in (1, 2) for z in (1, 2, gz)]
    y_side = [flat(x, gy, z) for x in (1, 2, gx) for z in (1, 2, gz)]
    return {"z": z_side, "x": x_side, "y": y_side}[which]


def own_sites():
    return [flat(x, y, z) for x, y, z in OWN]


def place_tiles(cells, spread, x, y, z):
    at = J_TILES * flat(x, y, z)
    spread[at + JX] = wide(4.0 * (cells[x, y, z, 0:1, :] + float(x)))
    spread[at + JY] = wide(4.0 * (cells[x, y, z, 1:2, :] + float(y)))
    spread[at + JZ] = wide(4.0 * (cells[x, y, z, 2:3, :] + float(z)))
    spread[at + JM] = wide(cells[x, y, z, 3:4, :])


def motion_tiles(cells, spread, x, y, z):
    at = J_TILES * flat(x, y, z)
    tile = cells[x, y, z]
    h4 = 4.0 * tile[7:8]
    spread[at + JU] = wide(40.0 * tile[4:5])
    spread[at + JV] = wide(40.0 * tile[5:6])
    spread[at + JW] = wide(40.0 * tile[6:7])
    spread[at + JH] = wide(h4)
    spread[at + JE] = wide(0.05 * h4)
    spread[at + JB] = wide(tile[3:4] * strength(h4))


def state_tiles(rho, fac, states, site):
    at = S_TILES * site
    states[at + JR] = wide(rho)
    states[at + JF] = wide(8.0 * fac)
    states[at + JS] = wide(jnp.sqrt((5.0 / 3.0) * fac * rho))


def gather_kernel(
    sizes,
    offsets_in,
    velocities_in,
    smoothing_in,
    mass_in,
    entropy_in,
    prior_in,
    active_in,
    spread,
    particles,
    partial,
    gas,
    ranks,
    density,
    offsets,
    velocities,
    smoothing,
    mass,
    entropy,
    prior,
    active,
    cells,
    own_states,
    sums,
    picked,
    load_sem,
    send_sem,
    recv_sem,
    send2_sem,
    recv2_sem,
):
    barrier = pltpu.get_barrier_semaphore()
    for step in AROUND:
        pl.semaphore_signal(
            barrier, inc=1, device_id=device_at(step, sizes), device_id_type=MESH
        )
    loads = [
        pltpu.make_async_copy(source, target, load_sem.at[index])
        for index, (source, target) in enumerate(
            (
                (offsets_in, offsets),
                (velocities_in, velocities),
                (smoothing_in, smoothing),
                (mass_in, mass),
                (entropy_in, entropy),
                (prior_in, prior),
                (active_in, active),
            )
        )
    ]
    for load in loads:
        load.start()
    for load in loads:
        load.wait()

    for c, (x, y, z) in enumerate(OWN):
        rows = [offsets[8 * d + c : 8 * d + c + 1] for d in range(3)]
        rows += [mass[c : c + 1]]
        rows += [velocities[8 * d + c : 8 * d + c + 1] for d in range(3)]
        rows += [smoothing[c : c + 1]]
        for row, value in enumerate(rows):
            cells[x, y, z, row : row + 1, :] = value
    pl.semaphore_wait(barrier, COUNT)
    copies = send_all(cells, sizes, send_sem, recv_sem)

    for x, y, z in OWN:
        place_tiles(cells, spread, x, y, z)
        motion_tiles(cells, spread, x, y, z)
    ranks[...] = ranks_of(active[...])

    for c, (x, y, z) in enumerate(OWN):
        tile = cells[x, y, z]
        h4 = 4.0 * tile[7:8]
        picked[0:1, :] = 4.0 * (tile[0:1] + float(x))
        picked[1:2, :] = 4.0 * (tile[1:2] + float(y))
        picked[2:3, :] = 4.0 * (tile[2:3] + float(z))
        picked[3:4, :] = h4
        picked[4:7, :] = 40.0 * tile[4:7]
        picked[7:8, :] = 0.05 * h4
        picked[8:9, :] = strength(h4)
        picked[9:10, :] = entropy[c : c + 1]
        picked[10:16, :] = jnp.zeros((6, LANES), F32)
        places = lax.broadcasted_iota(jnp.int32, (LANES, LANES), 0).astype(F32)
        found = places == jnp.broadcast_to(ranks[c : c + 1], (LANES, LANES))
        columns = lax.dot_general(
            jnp.where(found, 1.0, 0.0),
            picked[...],
            (((1,), (1,)), ((), ())),
            precision=lax.Precision.HIGHEST,
            preferred_element_type=F32,
        )
        for group in range(GROUPS):
            at = I_TILES * (GROUPS * c + group)
            for source, target in enumerate((IX, IY, IZ, IH, IU, IV, IW, IE, IB, IF)):
                particles[at + target] = jnp.broadcast_to(
                    columns[8 * group : 8 * group + 8, source : source + 1], (8, LANES)
                )

    def density_inputs(t):
        at = I_TILES * t
        return [particles[at + k] for k in (IX, IY, IZ, IH)]

    def inner_density(quad, carry):
        zero = jnp.zeros((8, LANES), F32)
        some = [4 * quad + k for k in range(4)]
        accs = density_sum([density_inputs(t) for t in some], spread, own_sites(), [zero] * 4)
        for t, acc in zip(some, accs):
            sums[t] = acc
        return carry

    lax.fori_loop(0, 2 * GROUPS, inner_density, 0)

    for which in ("z", "x", "y"):
        axis = {"z": 2, "x": 0, "y": 1}[which]
        later = {"z": (0, 1), "x": (1,), "y": ()}[which]
        for step in AROUND:
            if step[axis] and not any(step[k] for k in later):
                copies[step].wait_recv()
        for x, y, z in GHOST:
            cell = (x, y, z)
            if cell[axis] in (0, 3) and not any(cell[k] in (0, 3) for k in later):
                place_tiles(cells, spread, x, y, z)

        for c in range(8):
            sites = ghost_sites(c, which)

            def outer_density(quad, carry, c=c, sites=sites):
                some = [GROUPS * c + 4 * quad + k for k in range(4)]
                accs = density_sum(
                    [density_inputs(t) for t in some], spread, sites, [sums[t] for t in some]
                )
                for t, acc in zip(some, accs):
                    sums[t] = acc
                return carry

            lax.fori_loop(0, GROUPS // 4, outer_density, 0)

    def settle(c, carry):
        total = jnp.zeros((8, LANES), F32)
        for group in range(GROUPS):
            t = GROUPS * c + group
            at = I_TILES * t
            mask = chosen(ranks, c, group)
            rho = across(sums[t]) * (0.1 * particles[at + IB])
            total = total + jnp.where(mask, rho, 0.0)
            fac = particles[at + IF] * jnp.exp(jnp.log(rho) * (-1.0 / 3.0))
            particles[at + IR] = rho
            particles[at + IF] = 8.0 * fac
            particles[at + IS] = jnp.sqrt((5.0 / 3.0) * fac * rho)
        density[pl.ds(c, 1), :] = jnp.sum(total, axis=0, keepdims=True)
        return carry

    lax.fori_loop(0, 8, settle, 0)
    rho = jnp.where(active[...] == 1, density[...], prior[...])
    density[...] = rho
    fac = entropy[...] * jnp.exp(jnp.log(rho) * (-1.0 / 3.0))
    for c, (x, y, z) in enumerate(OWN):
        gas[x, y, z, 0:1, :] = rho[c : c + 1]
        gas[x, y, z, 1:2, :] = fac[c : c + 1]
    copies2 = send_all(gas, sizes, send2_sem, recv2_sem)

    for c, (x, y, z) in enumerate(OWN):
        state_tiles(rho[c : c + 1], fac[c : c + 1], own_states, flat(x, y, z))

    def inner_force(t, carry):
        at = I_TILES * t
        zero = jnp.zeros((8, LANES), F32)
        acc = force_sum(
            [particles[at + k] for k in range(I_TILES)],
            spread,
            own_states,
            own_sites(),
            (zero, zero, zero),
        )
        for d in range(3):
            partial[3 * t + d] = acc[d]
        return carry

    lax.fori_loop(0, 8 * GROUPS, inner_force, 0, unroll=2)
    for x, y, z in GHOST:
        motion_tiles(cells, spread, x, y, z)
    for step in AROUND:
        copies[step].wait_send()
        copies2[step].wait()


def force_kernel(
    spread, particles, partial, gas, ranks, density_in, density, accel, states, sums, counts
):
    density[...] = density_in[...]
    last = jnp.max(ranks[...], axis=1, keepdims=True)
    for c in range(8):
        counts[c] = (jnp.max(last[c : c + 1]) + 1.0).astype(jnp.int32)

    def prepare(site, carry):
        state_tiles(gas[site, 0:1, :], gas[site, 1:2, :], states, site)
        return carry

    lax.fori_loop(0, 64, prepare, 0, unroll=4)

    zero = jnp.zeros((8, LANES), F32)
    for c in range(8):
        groups = (counts[c] + 7) // 8
        sites = [site for which in ("z", "x", "y") for site in ghost_sites(c, which)]

        def group_step(group, inner, c=c, sites=sites):
            t = GROUPS * c + group
            at = I_TILES * t
            acc = force_sum(
                [particles[at + k] for k in range(I_TILES)],
                spread,
                states,
                sites,
                tuple(partial[3 * t + d] for d in range(3)),
            )
            for d in range(3):
                sums[3 * group + d] = acc[d]
            return inner

        lax.fori_loop(0, groups, group_step, 0)

        def fold(quad, totals, c=c):
            for k in range(4):
                group = 4 * quad + k
                mask = chosen(ranks, c, group)
                totals = tuple(
                    total + jnp.where(mask, across(sums[3 * group + d]), 0.0)
                    for d, total in enumerate(totals)
                )
            return totals

        totals = lax.fori_loop(0, (groups + 3) // 4, fold, (zero, zero, zero))
        for d in range(3):
            accel[8 * d + c : 8 * d + c + 1, :] = 0.25 * jnp.sum(totals[d], axis=0, keepdims=True)


def vmem(count):
    return [pl.BlockSpec(memory_space=pltpu.VMEM)] * count


def tiles(count):
    return jax.ShapeDtypeStruct((count, 8, LANES), F32)


def body(sizes, *args):
    rows = [pltpu.with_memory_space_constraint(a.reshape(-1, LANES), pltpu.HBM) for a in args]
    cell_rows = jax.ShapeDtypeStruct((8, LANES), F32)
    spread, particles, partial, gas, ranks, density = pl.pallas_call(
        functools.partial(gather_kernel, sizes),
        out_shape=(
            tiles(64 * J_TILES),
            tiles(8 * GROUPS * I_TILES),
            tiles(8 * GROUPS * 3),
            jax.ShapeDtypeStruct((4, 4, 4, 2, LANES), F32),
            cell_rows,
            cell_rows,
        ),
        in_specs=[pl.BlockSpec(memory_space=pltpu.HBM)] * 7,
        out_specs=tuple(vmem(6)),
        scratch_shapes=[
            pltpu.VMEM((24, LANES), F32),
            pltpu.VMEM((24, LANES), F32),
            pltpu.VMEM((8, LANES), F32),
            pltpu.VMEM((8, LANES), F32),
            pltpu.VMEM((8, LANES), F32),
            pltpu.VMEM((8, LANES), F32),
            pltpu.VMEM((8, LANES), jnp.int32),
            pltpu.VMEM((4, 4, 4, 8, LANES), F32),
            pltpu.VMEM((64 * S_TILES, 8, LANES), F32),
            pltpu.VMEM((8 * GROUPS, 8, LANES), F32),
            pltpu.VMEM((16, LANES), F32),
            pltpu.SemaphoreType.DMA((7,)),
            pltpu.SemaphoreType.DMA((COUNT,)),
            pltpu.SemaphoreType.DMA((COUNT,)),
            pltpu.SemaphoreType.DMA((COUNT,)),
            pltpu.SemaphoreType.DMA((COUNT,)),
        ],
        compiler_params=pltpu.CompilerParams(
            collective_id=0, has_side_effects=True, vmem_limit_bytes=VMEM_BYTES
        ),
    )(*rows)
    density, accel = pl.pallas_call(
        force_kernel,
        out_shape=(cell_rows, jax.ShapeDtypeStruct((24, LANES), F32)),
        in_specs=vmem(6),
        out_specs=tuple(vmem(2)),
        scratch_shapes=[
            pltpu.VMEM((64 * S_TILES, 8, LANES), F32),
            pltpu.VMEM((GROUPS * 3, 8, LANES), F32),
            pltpu.SMEM((8,), jnp.int32),
        ],
        compiler_params=pltpu.CompilerParams(vmem_limit_bytes=VMEM_BYTES),
    )(spread, particles, partial, gas.reshape(64, 2, LANES), ranks, density)
    return density.reshape(2, 2, 2, LANES), accel.reshape(3, 2, 2, 2, LANES)


def solution(mesh):
    sizes = tuple(mesh.shape[axis] for axis in AXES)
    spec = P("gx", "gy", "gz", None)
    spec3 = P(None, "gx", "gy", "gz", None)
    return jax.shard_map(
        functools.partial(body, sizes),
        mesh=mesh,
        in_specs=(spec3, spec3, spec, spec, spec, spec, spec),
        out_specs=(spec, spec3),
        check_vma=False,
    )
```

```python
import functools
import math

import jax
import jax.numpy as jnp
from jax import lax
from jax.experimental import pallas as pl
from jax.experimental.pallas import tpu as pltpu
from jax.sharding import PartitionSpec as P

MESH = pl.DeviceIdType.MESH
AXES = ("gx", "gy", "gz")
KERNEL_NORM = 21.0 / (2.0 * math.pi)
F32 = jnp.float32
LANES = 128
VMEM_BYTES = 18 * 1024 * 1024
BF16 = jnp.bfloat16
PARTS = 64

AROUND = sorted(
    (
        (a, b, c)
        for a in (-1, 0, 1)
        for b in (-1, 0, 1)
        for c in (-1, 0, 1)
        if (a, b, c) != (0, 0, 0)
    ),
    key=lambda d: (-abs(d[1]), -abs(d[0]), -abs(d[2]), d),
)
COUNT = len(AROUND)
JX, JY, JZ, JM, JH, JE, JB = range(7)
J_TILES = 7
JR, JF, JS = range(3)
S_TILES = 3
IX, IY, IZ, IH, IE, IB, IQ, IR, IF, IS = range(10)
I_TILES = 10
GROUPS = 16
OWN = [(x, y, z) for x in (1, 2) for y in (1, 2) for z in (1, 2)]
GHOST = [
    (x, y, z)
    for x in range(4)
    for y in range(4)
    for z in range(4)
    if not (x in (1, 2) and y in (1, 2) and z in (1, 2))
]


def device_at(step, sizes):
    return tuple(
        lax.rem(lax.axis_index(axis) + (move + size), size) if move else lax.axis_index(axis)
        for axis, move, size in zip(AXES, step, sizes)
    )


def leaving(step):
    return tuple({0: pl.ds(1, 2), 1: pl.ds(2, 1), -1: pl.ds(1, 1)}[move] for move in step)


def arriving(step):
    return tuple({0: pl.ds(1, 2), 1: pl.ds(0, 1), -1: pl.ds(3, 1)}[move] for move in step)


def send_all(cells, sizes, send_sem, recv_sem):
    copies = {}
    for index, step in enumerate(AROUND):
        copies[step] = pltpu.make_async_remote_copy(
            src_ref=cells.at[leaving(step)],
            dst_ref=cells.at[arriving(step)],
            send_sem=send_sem.at[index],
            recv_sem=recv_sem.at[index],
            device_id=device_at(step, sizes),
            device_id_type=MESH,
        )
        copies[step].start()
    return copies


def flat(x, y, z):
    return 16 * x + 4 * y + z


def wide(row):
    return jnp.broadcast_to(row, (8, LANES))


def strength(h4):
    h2 = h4 * h4
    q = h2 * h2
    return (2.5 * KERNEL_NORM * 1024.0) / (q * q)


def ranks_of(active):
    live = active == 1
    ahead = lax.broadcasted_iota(jnp.int32, (LANES, LANES), 0) < lax.broadcasted_iota(
        jnp.int32, (LANES, LANES), 1
    )
    before = jnp.dot(
        jnp.where(live, 1.0, 0.0).astype(jnp.bfloat16),
        jnp.where(ahead, 1.0, 0.0).astype(jnp.bfloat16),
        preferred_element_type=F32,
    )
    return jnp.where(live, before, -100.0)


def chosen(ranks, c, group):
    places = lax.broadcasted_iota(jnp.int32, (8, LANES), 0) + 8 * group
    return wide(ranks[pl.ds(c, 1), :]) == places.astype(F32)


def across(tile):
    return jnp.broadcast_to(jnp.sum(tile, axis=1, keepdims=True), (8, LANES))


def force_sum(own, spread, states, pairs, acc):
    x, y, z, h4, e4, b, _, rho, fac, sound = own
    ax, ay, az = acc
    for site, r4, app in pairs:
        j = J_TILES * site
        s = S_TILES * site
        near = jnp.maximum(h4 - r4, 0.0)
        far = jnp.maximum(spread[j + JH] - r4, 0.0)
        e = e4 + spread[j + JE]
        m = e * jnp.minimum(app, 0.0) / (r4 * r4 + e * e)
        visc = m * (m - (sound + states[s + JS])) / (rho + states[s + JR])
        g_near = (near * near) * (near * (b * spread[j + JM]))
        g_far = (far * far) * (far * spread[j + JB])
        w = (fac + visc) * g_near + (states[s + JF] + visc) * g_far
        ax = ax + w * (x - spread[j + JX])
        ay = ay + w * (y - spread[j + JY])
        az = az + w * (z - spread[j + JZ])
    return ax, ay, az


STAGES = {"z": (0, 4), "x": (32, 6), "y": (80, 9)}
PAIRS = 152


def own_site(k):
    return flat(1 + k // 4, 1 + (k // 2) % 2, 1 + k % 2)


def ghost_site(which, c, k):
    gx, gy, gz = 3 * (c // 4), 3 * ((c // 2) % 2), 3 * (c % 2)
    if which == "z":
        return flat(1 + k // 2, 1 + k % 2, gz)
    last = k % 3
    z = 1 + last + (last // 2) * (gz - 3)
    if which == "x":
        return flat(gx, 1 + k // 3, z)
    first = k // 3
    return flat(1 + first + (first // 2) * (gx - 3), gy, z)


def split(tile):
    one = tile.astype(BF16).astype(F32)
    two = (tile - one).astype(BF16).astype(F32)
    three = (tile - one - two).astype(BF16).astype(F32)
    return one, two, three


def stack(blocks):
    return jnp.concatenate(blocks, axis=0).astype(BF16)


def far_features(cells, features, right, x, y, z):
    site = flat(x, y, z)
    px = 4.0 * (cells[x, y, z, 0:1, :] + float(x - 2))
    py = 4.0 * (cells[x, y, z, 1:2, :] + float(y - 2))
    pz = 4.0 * (cells[x, y, z, 2:3, :] + float(z - 2))
    vx = 40.0 * cells[x, y, z, 3:4, :]
    vy = 40.0 * cells[x, y, z, 4:5, :]
    vz = 40.0 * cells[x, y, z, 5:6, :]
    rows = (px, py, pz, vx, vy, vz, px * px + py * py + pz * pz, px * vx + py * vy + pz * vz)
    for k, row in enumerate(rows):
        features[site, k : k + 1, :] = row
    one, two, three = split(features[site])
    index = lax.broadcasted_iota(jnp.int32, (8, LANES), 0)
    ones = jnp.where(index < 3, 1.0, 0.0)
    zero = jnp.zeros((8, LANES), F32)
    right[site, 0:16, :] = stack([one, one])
    right[site, 16:32, :] = stack([one, two])
    right[site, 32:48, :] = stack([two, three])
    right[site, 48:64, :] = stack([ones, zero])


def near_features(features, site):
    tile = features[site]
    px, py, pz, vx, vy, vz, square, dot = (tile[k : k + 1] for k in range(8))
    none = jnp.zeros((1, LANES), F32)
    one = jnp.ones((1, LANES), F32)
    zero = jnp.zeros((8, LANES), F32)
    result = []
    for rows, own in (
        ((-2.0 * px, -2.0 * py, -2.0 * pz, none, none, none, one, none), square),
        ((-vx, -vy, -vz, -px, -py, -pz, none, one), dot),
    ):
        u1, u2, u3 = split(jnp.concatenate(rows, axis=0))
        q = jnp.concatenate(list(split(own)) + [none] * 5, axis=0)
        result += [u1, u2, u3, u1, u2, u1, q, zero]
    return stack(result)


def place_tiles(cells, spread, x, y, z):
    at = J_TILES * flat(x, y, z)
    spread[at + JX] = wide(4.0 * (cells[x, y, z, 0:1, :] + float(x)))
    spread[at + JY] = wide(4.0 * (cells[x, y, z, 1:2, :] + float(y)))
    spread[at + JZ] = wide(4.0 * (cells[x, y, z, 2:3, :] + float(z)))
    h4 = 4.0 * cells[x, y, z, 7:8, :]
    spread[at + JH] = wide(h4)
    spread[at + JE] = wide(0.05 * h4)
    spread[at + JB] = wide(cells[x, y, z, 6:7, :] * strength(h4))


def mass_tile(cells, spread, x, y, z):
    spread[J_TILES * flat(x, y, z) + JM] = wide(cells[x, y, z, 6:7, :])


def state_tiles(rho, fac, states, site):
    at = S_TILES * site
    states[at + JR] = wide(rho)
    states[at + JF] = wide(8.0 * fac)
    states[at + JS] = wide(jnp.sqrt((5.0 / 3.0) * fac * rho))


def gather_kernel(
    sizes,
    offsets_in,
    velocities_in,
    smoothing_in,
    mass_in,
    entropy_in,
    prior_in,
    active_in,
    spread,
    particles,
    partial,
    gas,
    ranks,
    density,
    roots,
    approach,
    offsets,
    velocities,
    smoothing,
    mass,
    entropy,
    prior,
    active,
    cells,
    own_states,
    sums,
    picked,
    features,
    left,
    right,
    even,
    odd,
    own_roots,
    own_approach,
    load_sem,
    send_sem,
    recv_sem,
    send2_sem,
    recv2_sem,
):
    barrier = pltpu.get_barrier_semaphore()
    for step in AROUND:
        pl.semaphore_signal(
            barrier, inc=1, device_id=device_at(step, sizes), device_id_type=MESH
        )
    loads = [
        pltpu.make_async_copy(source, target, load_sem.at[index])
        for index, (source, target) in enumerate(
            (
                (offsets_in, offsets),
                (velocities_in, velocities),
                (smoothing_in, smoothing),
                (mass_in, mass),
                (entropy_in, entropy),
                (prior_in, prior),
                (active_in, active),
            )
        )
    ]
    for load in loads:
        load.start()
    for load in loads:
        load.wait()

    for c, (x, y, z) in enumerate(OWN):
        rows = [offsets[8 * d + c : 8 * d + c + 1] for d in range(3)]
        rows += [velocities[8 * d + c : 8 * d + c + 1] for d in range(3)]
        rows += [mass[c : c + 1], smoothing[c : c + 1]]
        for row, value in enumerate(rows):
            cells[x, y, z, row : row + 1, :] = value
    pl.semaphore_wait(barrier, COUNT)
    copies = send_all(cells, sizes, send_sem, recv_sem)

    for x, y, z in OWN:
        place_tiles(cells, spread, x, y, z)
        mass_tile(cells, spread, x, y, z)
        far_features(cells, features, right, x, y, z)
    ranks[...] = ranks_of(active[...])

    for c, (x, y, z) in enumerate(OWN):
        tile = cells[x, y, z]
        h4 = 4.0 * tile[7:8]
        picked[0:1, :] = 4.0 * (tile[0:1] + float(x))
        picked[1:2, :] = 4.0 * (tile[1:2] + float(y))
        picked[2:3, :] = 4.0 * (tile[2:3] + float(z))
        picked[3:4, :] = h4
        picked[4:5, :] = 0.05 * h4
        picked[5:6, :] = strength(h4)
        picked[6:7, :] = 0.25 * h4
        picked[7:8, :] = entropy[c : c + 1]
        places = lax.broadcasted_iota(jnp.int32, (LANES, LANES), 0).astype(F32)
        found = places == jnp.broadcast_to(ranks[c : c + 1], (LANES, LANES))
        found = jnp.where(found, 1.0, 0.0)
        near = lax.dot_general(
            found.astype(BF16),
            near_features(features, flat(x, y, z)),
            (((1,), (1,)), ((), ())),
            preferred_element_type=F32,
        )
        left[c, 0:LANES, :] = near[:, 0:PARTS].astype(BF16)
        left[c, LANES : 2 * LANES, :] = near[:, PARTS : 2 * PARTS].astype(BF16)
        columns = lax.dot_general(
            found,
            picked[...],
            (((1,), (1,)), ((), ())),
            precision=lax.Precision.HIGHEST,
            preferred_element_type=F32,
        )
        for group in range(GROUPS):
            at = I_TILES * (GROUPS * c + group)
            for source, target in enumerate((IX, IY, IZ, IH, IE, IB, IQ, IF)):
                particles[at + target] = jnp.broadcast_to(
                    columns[8 * group : 8 * group + 8, source : source + 1], (8, LANES)
                )

    def clear(t, carry):
        sums[t] = jnp.zeros((8, LANES), F32)
        return carry

    lax.fori_loop(0, 8 * GROUPS, clear, 0, unroll=8)

    def density_stage(per_cell, site_of, base, root_out, approach_out):
        total = 8 * per_cell

        def products(pair, target):
            c = pair // per_cell
            both = jnp.dot(
                left[c], right[site_of(c, pair % per_cell)], preferred_element_type=F32
            )
            target[...] = both[0:LANES]
            approach_out[base + pair] = both[LANES : 2 * LANES]

        def density_of(pair, source):
            c = pair // per_cell
            mass_j = spread[J_TILES * site_of(c, pair % per_cell) + JM]
            for group in range(GROUPS):
                t = GROUPS * c + group
                rows = slice(8 * group, 8 * group + 8)
                square = jnp.maximum(source[rows, :], 1e-12)
                r4 = square * lax.rsqrt(square)
                root_out[base + pair, rows, :] = r4
                u = jnp.maximum(particles[I_TILES * t + IH] - r4, 0.0)
                u2 = u * u
                sums[t] += (u2 * u2) * ((particles[I_TILES * t + IQ] + r4) * mass_j)

        products(0, even)

        def step(half, carry):
            products(2 * half + 1, odd)
            density_of(2 * half, even)
            products((2 * half + 2) % total, even)
            density_of(2 * half + 1, odd)
            return carry

        lax.fori_loop(0, total // 2, step, 0)

    density_stage(8, lambda c, k: own_site(k), 0, own_roots, own_approach)

    for which in ("z", "x", "y"):
        axis = {"z": 2, "x": 0, "y": 1}[which]
        later = {"z": (0, 1), "x": (1,), "y": ()}[which]
        for step in AROUND:
            if step[axis] and not any(step[k] for k in later):
                copies[step].wait_recv()
        for x, y, z in GHOST:
            cell = (x, y, z)
            if cell[axis] in (0, 3) and not any(cell[k] in (0, 3) for k in later):
                mass_tile(cells, spread, x, y, z)
                far_features(cells, features, right, x, y, z)
        base, per_cell = STAGES[which]
        density_stage(per_cell, functools.partial(ghost_site, which), base, roots, approach)

    for c in range(8):
        total = jnp.zeros((8, LANES), F32)
        for group in range(GROUPS):
            t = GROUPS * c + group
            rho = across(sums[t]) * (0.1 * particles[I_TILES * t + IB])
            particles[I_TILES * t + IR] = rho
            total = total + jnp.where(chosen(ranks, c, group), rho, 0.0)
        density[c : c + 1, :] = jnp.sum(total, axis=0, keepdims=True)
    rho = jnp.where(active[...] == 1, density[...], prior[...])
    density[...] = rho
    fac = entropy[...] * jnp.exp(jnp.log(rho) * (-1.0 / 3.0))
    for c, (x, y, z) in enumerate(OWN):
        gas[x, y, z, 0:1, :] = rho[c : c + 1]
        gas[x, y, z, 1:2, :] = fac[c : c + 1]
    copies2 = send_all(gas, sizes, send2_sem, recv2_sem)

    def settle(t, carry):
        at = I_TILES * t
        rho_i = particles[at + IR]
        fac_i = particles[at + IF] * jnp.exp(jnp.log(rho_i) * (-1.0 / 3.0))
        particles[at + IF] = 8.0 * fac_i
        particles[at + IS] = jnp.sqrt((5.0 / 3.0) * fac_i * rho_i)
        return carry

    lax.fori_loop(0, 8 * GROUPS, settle, 0, unroll=8)

    for c, (x, y, z) in enumerate(OWN):
        state_tiles(rho[c : c + 1], fac[c : c + 1], own_states, flat(x, y, z))

    def inner_force(t, carry):
        at = I_TILES * t
        rows = pl.ds(8 * (t % GROUPS), 8)
        zero = jnp.zeros((8, LANES), F32)
        acc = force_sum(
            [particles[at + k] for k in range(I_TILES)],
            spread,
            own_states,
            [
                (
                    own_site(k),
                    own_roots[8 * (t // GROUPS) + k, rows, :],
                    own_approach[8 * (t // GROUPS) + k, rows, :],
                )
                for k in range(8)
            ],
            (zero, zero, zero),
        )
        for d in range(3):
            partial[3 * t + d] = acc[d]
        return carry

    lax.fori_loop(0, 8 * GROUPS, inner_force, 0, unroll=2)
    for x, y, z in GHOST:
        place_tiles(cells, spread, x, y, z)
    for step in AROUND:
        copies[step].wait_send()
        copies2[step].wait()


def force_kernel(
    spread,
    particles,
    partial,
    gas,
    ranks,
    density_in,
    roots,
    approach,
    density,
    accel,
    states,
    sums,
    counts,
):
    density[...] = density_in[...]
    last = jnp.max(ranks[...], axis=1, keepdims=True)
    for c in range(8):
        counts[c] = (jnp.maximum(jnp.max(last[c : c + 1]), -1.0) + 8.0).astype(jnp.int32) // 8

    def prepare(site, carry):
        state_tiles(gas[site, 0:1, :], gas[site, 1:2, :], states, site)
        return carry

    lax.fori_loop(0, 64, prepare, 0, unroll=4)

    zero = jnp.zeros((8, LANES), F32)
    sums[...] = jnp.zeros(sums.shape, F32)

    def fold(c, group, totals):
        mask = chosen(ranks, c, group)
        at = 3 * (GROUPS * c + jnp.maximum(group, 0))
        return tuple(
            total + jnp.where(mask, across(sums[at + d]), 0.0) for d, total in enumerate(totals)
        )

    totals = []
    for c in range(8):
        pairs = [
            (ghost_site(which, c, k), base + per_cell * c + k)
            for which, (base, per_cell) in STAGES.items()
            for k in range(per_cell)
        ]

        def group_step(group, found, c=c, pairs=pairs):
            found = fold(c, group - 1, found)
            t = GROUPS * c + group
            rows = pl.ds(8 * group, 8)
            acc = force_sum(
                [particles[I_TILES * t + k] for k in range(I_TILES)],
                spread,
                states,
                [(site, roots[pair, rows, :], approach[pair, rows, :]) for site, pair in pairs],
                tuple(partial[3 * t + d] for d in range(3)),
            )
            for d in range(3):
                sums[3 * t + d] = acc[d]
            return found

        totals.append(lax.fori_loop(0, counts[c], group_step, (zero, zero, zero)))
    for c in range(8):
        found = fold(c, counts[c] - 1, totals[c])
        for d in range(3):
            accel[8 * d + c : 8 * d + c + 1, :] = 0.25 * jnp.sum(found[d], axis=0, keepdims=True)


def vmem(count):
    return [pl.BlockSpec(memory_space=pltpu.VMEM)] * count


def tiles(count):
    return jax.ShapeDtypeStruct((count, 8, LANES), F32)


def body(sizes, *args):
    rows = [pltpu.with_memory_space_constraint(a.reshape(-1, LANES), pltpu.HBM) for a in args]
    cell_rows = jax.ShapeDtypeStruct((8, LANES), F32)
    spread, particles, partial, gas, ranks, density, roots, approach = pl.pallas_call(
        functools.partial(gather_kernel, sizes),
        out_shape=(
            tiles(64 * J_TILES),
            tiles(8 * GROUPS * I_TILES),
            tiles(8 * GROUPS * 3),
            jax.ShapeDtypeStruct((4, 4, 4, 2, LANES), F32),
            cell_rows,
            cell_rows,
            jax.ShapeDtypeStruct((PAIRS, LANES, LANES), F32),
            jax.ShapeDtypeStruct((PAIRS, LANES, LANES), F32),
        ),
        in_specs=[pl.BlockSpec(memory_space=pltpu.HBM)] * 7,
        out_specs=tuple(vmem(8)),
        scratch_shapes=[
            pltpu.VMEM((24, LANES), F32),
            pltpu.VMEM((24, LANES), F32),
            pltpu.VMEM((8, LANES), F32),
            pltpu.VMEM((8, LANES), F32),
            pltpu.VMEM((8, LANES), F32),
            pltpu.VMEM((8, LANES), F32),
            pltpu.VMEM((8, LANES), jnp.int32),
            pltpu.VMEM((4, 4, 4, 8, LANES), F32),
            pltpu.VMEM((64 * S_TILES, 8, LANES), F32),
            pltpu.VMEM((8 * GROUPS, 8, LANES), F32),
            pltpu.VMEM((8, LANES), F32),
            pltpu.VMEM((64, 8, LANES), F32),
            pltpu.VMEM((8, 2 * LANES, PARTS), BF16),
            pltpu.VMEM((64, PARTS, LANES), BF16),
            pltpu.VMEM((LANES, LANES), F32),
            pltpu.VMEM((LANES, LANES), F32),
            pltpu.VMEM((64, LANES, LANES), F32),
            pltpu.VMEM((64, LANES, LANES), F32),
            pltpu.SemaphoreType.DMA((7,)),
            pltpu.SemaphoreType.DMA((COUNT,)),
            pltpu.SemaphoreType.DMA((COUNT,)),
            pltpu.SemaphoreType.DMA((COUNT,)),
            pltpu.SemaphoreType.DMA((COUNT,)),
        ],
        compiler_params=pltpu.CompilerParams(
            collective_id=0, has_side_effects=True, vmem_limit_bytes=VMEM_BYTES
        ),
    )(*rows)
    density, accel = pl.pallas_call(
        force_kernel,
        out_shape=(cell_rows, jax.ShapeDtypeStruct((24, LANES), F32)),
        in_specs=vmem(8),
        out_specs=tuple(vmem(2)),
        scratch_shapes=[
            pltpu.VMEM((64 * S_TILES, 8, LANES), F32),
            pltpu.VMEM((8 * GROUPS * 3, 8, LANES), F32),
            pltpu.SMEM((8,), jnp.int32),
        ],
        compiler_params=pltpu.CompilerParams(vmem_limit_bytes=VMEM_BYTES),
    )(spread, particles, partial, gas.reshape(64, 2, LANES), ranks, density, roots, approach)
    return density.reshape(2, 2, 2, LANES), accel.reshape(3, 2, 2, 2, LANES)


def solution(mesh):
    sizes = tuple(mesh.shape[axis] for axis in AXES)
    spec = P("gx", "gy", "gz", None)
    spec3 = P(None, "gx", "gy", "gz", None)
    return jax.shard_map(
        functools.partial(body, sizes),
        mesh=mesh,
        in_specs=(spec3, spec3, spec, spec, spec, spec, spec),
        out_specs=(spec, spec3),
        check_vma=False,
    )
```

```python
import functools
import math

import jax
import jax.numpy as jnp
from jax import lax
from jax.experimental import pallas as pl
from jax.experimental.pallas import tpu as pltpu
from jax.sharding import PartitionSpec as P

MESH = pl.DeviceIdType.MESH
AXES = ("gx", "gy", "gz")
KERNEL_NORM = 21.0 / (2.0 * math.pi)
F32 = jnp.float32
LANES = 128
VMEM_BYTES = 16 * 1024 * 1024

AROUND = sorted(
    (
        (a, b, c)
        for a in (-1, 0, 1)
        for b in (-1, 0, 1)
        for c in (-1, 0, 1)
        if (a, b, c) != (0, 0, 0)
    ),
    key=lambda d: (-abs(d[1]), -abs(d[0]), -abs(d[2]), d),
)
COUNT = len(AROUND)
JX, JY, JZ, JM, JU, JV, JW, JH, JE, JB = range(10)
J_TILES = 10
JR, JF, JS = range(3)
S_TILES = 3
IX, IY, IZ, IH, IU, IV, IW, IE, IB, IR, IF, IS = range(12)
I_TILES = 12
FIELDS = (IX, IY, IZ, IH, IU, IV, IW, IE, IB, IF)
GROUPS = 16
READY = 8
STAGES = {"z": (0, 4), "x": (32, 6), "y": (80, 6), "w": (128, 3)}
PAIRS = 152
STEPS = [16 * a + 4 * b + c for a in (-1, 0, 1) for b in (-1, 0, 1) for c in (-1, 0, 1)]
OWN = [(x, y, z) for x in (1, 2) for y in (1, 2) for z in (1, 2)]
GHOST = [
    (x, y, z)
    for x in range(4)
    for y in range(4)
    for z in range(4)
    if not (x in (1, 2) and y in (1, 2) and z in (1, 2))
]


def device_at(step, sizes):
    return tuple(
        lax.rem(lax.axis_index(axis) + (move + size), size) if move else lax.axis_index(axis)
        for axis, move, size in zip(AXES, step, sizes)
    )


def leaving(step):
    return tuple({0: pl.ds(1, 2), 1: pl.ds(2, 1), -1: pl.ds(1, 1)}[move] for move in step)


def arriving(step):
    return tuple({0: pl.ds(1, 2), 1: pl.ds(0, 1), -1: pl.ds(3, 1)}[move] for move in step)


def send_all(cells, sizes, send_sem, recv_sem):
    copies = {}
    for index, step in enumerate(AROUND):
        copies[step] = pltpu.make_async_remote_copy(
            src_ref=cells.at[leaving(step)],
            dst_ref=cells.at[arriving(step)],
            send_sem=send_sem.at[index],
            recv_sem=recv_sem.at[index],
            device_id=device_at(step, sizes),
            device_id_type=MESH,
        )
        copies[step].start()
    return copies


def flat(x, y, z):
    return 16 * x + 4 * y + z


def wide(row):
    return jnp.broadcast_to(row, (8, LANES))


def strength(h4):
    h2 = h4 * h4
    q = h2 * h2
    return (2.5 * KERNEL_NORM * 1024.0) / (q * q)


def ranks_of(active):
    live = active == 1
    ahead = lax.broadcasted_iota(jnp.int32, (LANES, LANES), 0) < lax.broadcasted_iota(
        jnp.int32, (LANES, LANES), 1
    )
    before = jnp.dot(
        jnp.where(live, 1.0, 0.0).astype(jnp.bfloat16),
        jnp.where(ahead, 1.0, 0.0).astype(jnp.bfloat16),
        preferred_element_type=F32,
    )
    return jnp.where(live, before, -100.0)


def chosen(ranks, c, group):
    places = lax.broadcasted_iota(jnp.int32, (8, LANES), 0) + 8 * group
    return wide(ranks[pl.ds(c, 1), :]) == places.astype(F32)


def across(tile):
    return jnp.broadcast_to(jnp.sum(tile, axis=1, keepdims=True), (8, LANES))


def density_sum(owns, spread, sites, accs, keep):
    accs = list(accs)
    for index, site in enumerate(sites):
        j = J_TILES * site
        xj, yj, zj, mj = (spread[j + k] for k in (JX, JY, JZ, JM))
        for k, (x, y, z, h4) in enumerate(owns):
            dx = x - xj
            dy = y - yj
            dz = z - zj
            sq = dx * dx + dy * dy + dz * dz
            r4 = sq * lax.rsqrt(jnp.maximum(sq, 1e-30))
            keep(index, k, r4)
            u = jnp.maximum(h4 - r4, 0.0)
            u2 = u * u
            accs[k] = accs[k] + (u2 * u2) * ((0.25 * h4 + r4) * mj)
    return accs


def closing_speed(own, other, sq):
    x, y, z, _, vx, vy, vz, e4 = own[:8]
    xj, yj, zj, uj, vj, wj, ej = other
    app = (x - xj) * (vx - uj) + (y - yj) * (vy - vj) + (z - zj) * (vz - wj)
    e = e4 + ej
    return e * jnp.minimum(app, 0.0) / (sq + e * e)


def motion_of(spread, site):
    return [spread[J_TILES * site + k] for k in (JX, JY, JZ, JU, JV, JW, JE)]


def force_sum(own, spread, states, pairs, acc):
    x, y, z, h4, _, _, _, _, b, rho, fac, sound = own
    ax, ay, az = acc
    for site, r4, m in pairs:
        j = J_TILES * site
        s = S_TILES * site
        dx = x - spread[j + JX]
        dy = y - spread[j + JY]
        dz = z - spread[j + JZ]
        if r4 is None:
            sq = dx * dx + dy * dy + dz * dz
            r4 = sq * lax.rsqrt(jnp.maximum(sq, 1e-30))
        if m is None:
            m = closing_speed(own, motion_of(spread, site), r4 * r4)
        near = jnp.maximum(h4 - r4, 0.0)
        far = jnp.maximum(spread[j + JH] - r4, 0.0)
        visc = m * (m - (sound + states[s + JS])) / (rho + states[s + JR])
        g_near = (near * near) * (near * (b * spread[j + JM]))
        g_far = (far * far) * (far * spread[j + JB])
        w = (fac + visc) * g_near + (states[s + JF] + visc) * g_far
        ax = ax + w * dx
        ay = ay + w * dy
        az = az + w * dz
    return ax, ay, az


def ghost_sites(c, which):
    gx, gy, gz = 3 * (c // 4), 3 * ((c // 2) % 2), 3 * (c % 2)
    z_side = [flat(x, y, gz) for x in (1, 2) for y in (1, 2)]
    x_side = [flat(gx, y, z) for y in (1, 2) for z in (1, 2, gz)]
    y_side = [flat(x, gy, z) for x in (1, 2) for z in (1, 2, gz)]
    w_side = [flat(gx, gy, z) for z in (1, 2, gz)]
    return {"z": z_side, "x": x_side, "y": y_side, "w": w_side}[which]


def stage_of(step):
    if step[1]:
        return "w" if step[0] else "y"
    return "x" if step[0] else "z"


def outside(place):
    return tuple(0 if k in (1, 2) else 1 for k in place)


def own_sites():
    return [flat(x, y, z) for x, y, z in OWN]


def place_tiles(cells, spread, x, y, z):
    at = J_TILES * flat(x, y, z)
    spread[at + JX] = wide(4.0 * (cells[x, y, z, 0:1, :] + float(x)))
    spread[at + JY] = wide(4.0 * (cells[x, y, z, 1:2, :] + float(y)))
    spread[at + JZ] = wide(4.0 * (cells[x, y, z, 2:3, :] + float(z)))
    spread[at + JM] = wide(cells[x, y, z, 3:4, :])


def motion_tiles(cells, spread, x, y, z):
    at = J_TILES * flat(x, y, z)
    tile = cells[x, y, z]
    h4 = 4.0 * tile[7:8]
    spread[at + JU] = wide(40.0 * tile[4:5])
    spread[at + JV] = wide(40.0 * tile[5:6])
    spread[at + JW] = wide(40.0 * tile[6:7])
    spread[at + JH] = wide(h4)
    spread[at + JE] = wide(0.05 * h4)
    spread[at + JB] = wide(tile[3:4] * strength(h4))


def state_tiles(rho, fac, states, site):
    at = S_TILES * site
    states[at + JR] = wide(rho)
    states[at + JF] = wide(8.0 * fac)
    states[at + JS] = wide(jnp.sqrt((5.0 / 3.0) * fac * rho))


def gather_kernel(
    sizes,
    offsets_in,
    velocities_in,
    smoothing_in,
    mass_in,
    entropy_in,
    prior_in,
    active_in,
    spread,
    particles,
    partial,
    gas,
    ranks,
    density,
    roots,
    slopes,
    offsets,
    velocities,
    smoothing,
    mass,
    entropy,
    prior,
    active,
    cells,
    own_states,
    sums,
    picked,
    columns,
    own_roots,
    load_sem,
    send_sem,
    recv_sem,
    send2_sem,
    recv2_sem,
):
    barrier = pltpu.get_barrier_semaphore()
    for step in AROUND:
        pl.semaphore_signal(
            barrier, inc=1, device_id=device_at(step, sizes), device_id_type=MESH
        )
    loads = [
        pltpu.make_async_copy(source, target, load_sem.at[index])
        for index, (source, target) in enumerate(
            (
                (offsets_in, offsets),
                (velocities_in, velocities),
                (smoothing_in, smoothing),
                (mass_in, mass),
                (entropy_in, entropy),
                (prior_in, prior),
                (active_in, active),
            )
        )
    ]
    for load in loads:
        load.start()
    for load in loads:
        load.wait()

    for c, (x, y, z) in enumerate(OWN):
        rows = [offsets[8 * d + c : 8 * d + c + 1] for d in range(3)]
        rows += [mass[c : c + 1]]
        rows += [velocities[8 * d + c : 8 * d + c + 1] for d in range(3)]
        rows += [smoothing[c : c + 1]]
        for row, value in enumerate(rows):
            cells[x, y, z, row : row + 1, :] = value
    pl.semaphore_wait(barrier, COUNT)
    copies = send_all(cells, sizes, send_sem, recv_sem)

    for x, y, z in OWN:
        place_tiles(cells, spread, x, y, z)
        motion_tiles(cells, spread, x, y, z)
    ranks[...] = ranks_of(active[...])

    def spread_columns(c, targets):
        for target in targets:
            source = FIELDS.index(target)
            for group in range(GROUPS):
                particles[I_TILES * (GROUPS * c + group) + target] = jnp.broadcast_to(
                    columns[c, 8 * group : 8 * group + 8, source : source + 1], (8, LANES)
                )

    for c, (x, y, z) in enumerate(OWN):
        tile = cells[x, y, z]
        h4 = 4.0 * tile[7:8]
        picked[0:1, :] = 4.0 * (tile[0:1] + float(x))
        picked[1:2, :] = 4.0 * (tile[1:2] + float(y))
        picked[2:3, :] = 4.0 * (tile[2:3] + float(z))
        picked[3:4, :] = h4
        picked[4:7, :] = 40.0 * tile[4:7]
        picked[7:8, :] = 0.05 * h4
        picked[8:9, :] = strength(h4)
        picked[9:10, :] = entropy[c : c + 1]
        picked[10:16, :] = jnp.zeros((6, LANES), F32)
        places = lax.broadcasted_iota(jnp.int32, (LANES, LANES), 0).astype(F32)
        found = places == jnp.broadcast_to(ranks[c : c + 1], (LANES, LANES))
        columns[c] = lax.dot_general(
            jnp.where(found, 1.0, 0.0),
            picked[...],
            (((1,), (1,)), ((), ())),
            precision=lax.Precision.HIGHEST,
            preferred_element_type=F32,
        )
        spread_columns(c, (IX, IY, IZ, IH))

    def density_inputs(t):
        at = I_TILES * t
        return [particles[at + k] for k in (IX, IY, IZ, IH)]

    zero = jnp.zeros((8, LANES), F32)

    def density_part(c, half, sites, first, target, fresh):
        some = [GROUPS * c + 8 * half + k for k in range(8)]

        def keep(index, k, value):
            target[first + index, pl.ds(pl.multiple_of(64 * half, 64) + 8 * k, 8), :] = value

        accs = density_sum(
            [density_inputs(t) for t in some],
            spread,
            sites,
            [zero] * 8 if fresh else [sums[t] for t in some],
            keep,
        )
        for t, acc in zip(some, accs):
            sums[t] = acc

    def inner_density(part, carry):
        c = part // 2
        density_part(c, part % 2, own_sites(), 8 * c, own_roots, True)
        return carry

    lax.fori_loop(0, GROUPS, inner_density, 0)

    for which, (base, per_cell) in STAGES.items():
        for step in AROUND:
            if stage_of(step) == which:
                copies[step].wait_recv()
        for x, y, z in GHOST:
            if stage_of(outside((x, y, z))) == which:
                place_tiles(cells, spread, x, y, z)
        for c in range(8):

            def outer_density(half, carry, c=c, which=which, first=base + per_cell * c):
                density_part(c, half, ghost_sites(c, which), first, roots, False)
                return carry

            lax.fori_loop(0, 2, outer_density, 0)

    for c in range(8):
        spread_columns(c, (IB,))
        total = zero
        for group in range(GROUPS):
            t = GROUPS * c + group
            rho = across(sums[t]) * (0.1 * particles[I_TILES * t + IB])
            particles[I_TILES * t + IR] = rho
            total = total + jnp.where(chosen(ranks, c, group), rho, 0.0)
        density[c : c + 1, :] = jnp.sum(total, axis=0, keepdims=True)
    rho = jnp.where(active[...] == 1, density[...], prior[...])
    density[...] = rho
    fac = entropy[...] * jnp.exp(jnp.log(rho) * (-1.0 / 3.0))
    for c, (x, y, z) in enumerate(OWN):
        gas[x, y, z, 0:1, :] = rho[c : c + 1]
        gas[x, y, z, 1:2, :] = fac[c : c + 1]
    copies2 = send_all(gas, sizes, send2_sem, recv2_sem)

    for c in range(8):
        spread_columns(c, (IU, IV, IW, IE, IF))

    def settle(t, carry):
        at = I_TILES * t
        rho_i = particles[at + IR]
        fac_i = particles[at + IF] * jnp.exp(jnp.log(rho_i) * (-1.0 / 3.0))
        particles[at + IF] = 8.0 * fac_i
        particles[at + IS] = jnp.sqrt((5.0 / 3.0) * fac_i * rho_i)
        return carry

    lax.fori_loop(0, 8 * GROUPS, settle, 0, unroll=8)

    for c, (x, y, z) in enumerate(OWN):
        state_tiles(rho[c : c + 1], fac[c : c + 1], own_states, flat(x, y, z))

    def inner_force(t, carry):
        c, group = t // READY, t % READY
        at = I_TILES * (GROUPS * c + group)
        rows = pl.ds(pl.multiple_of(8 * group, 8), 8)
        acc = force_sum(
            [particles[at + k] for k in range(I_TILES)],
            spread,
            own_states,
            [(site, own_roots[8 * c + k, rows, :], None) for k, site in enumerate(own_sites())],
            (zero, zero, zero),
        )
        for d in range(3):
            partial[3 * t + d] = acc[d]
        return carry

    lax.fori_loop(0, 8 * READY, inner_force, 0)
    for x, y, z in GHOST:
        motion_tiles(cells, spread, x, y, z)
    for c in range(8):
        pairs = [
            (site, base + per_cell * c + k)
            for which, (base, per_cell) in STAGES.items()
            for k, site in enumerate(ghost_sites(c, which))
        ]

        def slope(two, carry, c=c, pairs=pairs):
            owns = [
                [particles[I_TILES * (GROUPS * c + 2 * two + k) + f] for f in range(8)]
                for k in range(2)
            ]
            for site, pair in pairs:
                other = motion_of(spread, site)
                for k, own in enumerate(owns):
                    rows = pl.ds(pl.multiple_of(16 * two, 16) + 8 * k, 8)
                    r4 = roots[pair, rows, :]
                    slopes[pair, rows, :] = closing_speed(own, other, r4 * r4)
            return carry

        lax.fori_loop(0, READY // 2, slope, 0)
    for step in AROUND:
        copies[step].wait_send()
        copies2[step].wait()


def force_kernel(
    spread,
    particles,
    partial,
    gas,
    ranks,
    density_in,
    roots,
    slopes,
    density,
    accel,
    states,
    sums,
    counts,
):
    density[...] = density_in[...]
    last = jnp.max(ranks[...], axis=1, keepdims=True)
    for c in range(8):
        counts[c] = (jnp.maximum(jnp.max(last[c : c + 1]), -1.0) + 8.0).astype(jnp.int32) // 8

    def prepare(site, carry):
        state_tiles(gas[site, 0:1, :], gas[site, 1:2, :], states, site)
        return carry

    lax.fori_loop(0, 64, prepare, 0, unroll=4)

    zero = jnp.zeros((8, LANES), F32)
    nothing = (zero, zero, zero)

    def late_cell(c, carry):
        here = flat(1 + c // 4, 1 + (c // 2) % 2, 1 + c % 2)

        def late_group(group, found):
            at = I_TILES * (GROUPS * c + group)
            acc = force_sum(
                [particles[at + k] for k in range(I_TILES)],
                spread,
                states,
                [(here + step, None, None) for step in STEPS],
                nothing,
            )
            mask = chosen(ranks, c, group)
            return tuple(
                total + jnp.where(mask, across(part), 0.0) for total, part in zip(found, acc)
            )

        found = lax.fori_loop(READY, jnp.maximum(counts[c], READY), late_group, nothing)
        for d in range(3):
            accel[pl.ds(8 * d + c, 1), :] = jnp.sum(found[d], axis=0, keepdims=True)
        return carry

    lax.fori_loop(0, 8, late_cell, 0)
    sums[...] = jnp.zeros(sums.shape, F32)

    def fold(c, group, totals):
        mask = chosen(ranks, c, group)
        at = 3 * (READY * c + jnp.maximum(group, 0))
        return tuple(
            total + jnp.where(mask, across(sums[at + d]), 0.0) for d, total in enumerate(totals)
        )

    totals = []
    for c in range(8):
        pairs = [
            (site, base + per_cell * c + k)
            for which, (base, per_cell) in STAGES.items()
            for k, site in enumerate(ghost_sites(c, which))
        ]

        def group_step(group, found, c=c, pairs=pairs):
            found = fold(c, group - 1, found)
            at = I_TILES * (GROUPS * c + group)
            t = READY * c + group
            rows = pl.ds(pl.multiple_of(8 * group, 8), 8)
            acc = force_sum(
                [particles[at + k] for k in range(I_TILES)],
                spread,
                states,
                [(site, roots[pair, rows, :], slopes[pair, rows, :]) for site, pair in pairs],
                tuple(partial[3 * t + d] for d in range(3)),
            )
            for d in range(3):
                sums[3 * t + d] = acc[d]
            return found

        totals.append(lax.fori_loop(0, jnp.minimum(counts[c], READY), group_step, nothing))
    for c in range(8):
        found = fold(c, jnp.minimum(counts[c], READY) - 1, totals[c])
        for d in range(3):
            row = slice(8 * d + c, 8 * d + c + 1)
            accel[row, :] = 0.25 * (accel[row, :] + jnp.sum(found[d], axis=0, keepdims=True))


def vmem(count):
    return [pl.BlockSpec(memory_space=pltpu.VMEM)] * count


def tiles(count):
    return jax.ShapeDtypeStruct((count, 8, LANES), F32)


def body(sizes, *args):
    rows = [pltpu.with_memory_space_constraint(a.reshape(-1, LANES), pltpu.HBM) for a in args]
    cell_rows = jax.ShapeDtypeStruct((8, LANES), F32)
    spread, particles, partial, gas, ranks, density, roots, slopes = pl.pallas_call(
        functools.partial(gather_kernel, sizes),
        out_shape=(
            tiles(64 * J_TILES),
            tiles(8 * GROUPS * I_TILES),
            tiles(8 * READY * 3),
            jax.ShapeDtypeStruct((4, 4, 4, 2, LANES), F32),
            cell_rows,
            cell_rows,
            jax.ShapeDtypeStruct((PAIRS, LANES, LANES), F32),
            jax.ShapeDtypeStruct((PAIRS, 8 * READY, LANES), F32),
        ),
        in_specs=[pl.BlockSpec(memory_space=pltpu.HBM)] * 7,
        out_specs=tuple(vmem(8)),
        scratch_shapes=[
            pltpu.VMEM((24, LANES), F32),
            pltpu.VMEM((24, LANES), F32),
            pltpu.VMEM((8, LANES), F32),
            pltpu.VMEM((8, LANES), F32),
            pltpu.VMEM((8, LANES), F32),
            pltpu.VMEM((8, LANES), F32),
            pltpu.VMEM((8, LANES), jnp.int32),
            pltpu.VMEM((4, 4, 4, 8, LANES), F32),
            pltpu.VMEM((64 * S_TILES, 8, LANES), F32),
            pltpu.VMEM((8 * GROUPS, 8, LANES), F32),
            pltpu.VMEM((16, LANES), F32),
            pltpu.VMEM((8, LANES, 16), F32),
            pltpu.VMEM((64, LANES, LANES), F32),
            pltpu.SemaphoreType.DMA((7,)),
            pltpu.SemaphoreType.DMA((COUNT,)),
            pltpu.SemaphoreType.DMA((COUNT,)),
            pltpu.SemaphoreType.DMA((COUNT,)),
            pltpu.SemaphoreType.DMA((COUNT,)),
        ],
        compiler_params=pltpu.CompilerParams(
            collective_id=0, has_side_effects=True, vmem_limit_bytes=VMEM_BYTES
        ),
    )(*rows)
    density, accel = pl.pallas_call(
        force_kernel,
        out_shape=(cell_rows, jax.ShapeDtypeStruct((24, LANES), F32)),
        in_specs=vmem(8),
        out_specs=tuple(vmem(2)),
        scratch_shapes=[
            pltpu.VMEM((64 * S_TILES, 8, LANES), F32),
            pltpu.VMEM((8 * READY * 3, 8, LANES), F32),
            pltpu.SMEM((8,), jnp.int32),
        ],
        compiler_params=pltpu.CompilerParams(vmem_limit_bytes=VMEM_BYTES),
    )(spread, particles, partial, gas.reshape(64, 2, LANES), ranks, density, roots, slopes)
    return density.reshape(2, 2, 2, LANES), accel.reshape(3, 2, 2, 2, LANES)


def solution(mesh):
    sizes = tuple(mesh.shape[axis] for axis in AXES)
    spec = P("gx", "gy", "gz", None)
    spec3 = P(None, "gx", "gy", "gz", None)
    return jax.shard_map(
        functools.partial(body, sizes),
        mesh=mesh,
        in_specs=(spec3, spec3, spec, spec, spec, spec, spec),
        out_specs=(spec, spec3),
        check_vma=False,
    )
```

```python
import functools
import math

import jax
import jax.numpy as jnp
from jax import lax
from jax.experimental import pallas as pl
from jax.experimental.pallas import tpu as pltpu
from jax.sharding import PartitionSpec as P

MESH = pl.DeviceIdType.MESH
AXES = ("gx", "gy", "gz")
KERNEL_NORM = 21.0 / (2.0 * math.pi)
F32 = jnp.float32
LANES = 128
VMEM_BYTES = 16 * 1024 * 1024

AROUND = sorted(
    (
        (a, b, c)
        for a in (-1, 0, 1)
        for b in (-1, 0, 1)
        for c in (-1, 0, 1)
        if (a, b, c) != (0, 0, 0)
    ),
    key=lambda d: (-abs(d[1]), -abs(d[0]), -abs(d[2]), d),
)
COUNT = len(AROUND)
JX, JY, JZ, JM, JU, JV, JW, JH, JE, JB = range(10)
J_TILES = 10
JR, JF, JS = range(3)
S_TILES = 3
IX, IY, IZ, IH, IU, IV, IW, IE, IB, IR, IF, IS = range(12)
I_TILES = 12
FIELDS = (IX, IY, IZ, IH, IU, IV, IW, IB, IF)
GROUPS = 16
READY = 8
STAGES = {"z": (0, 4), "x": (32, 6), "y": (80, 6), "w": (128, 3)}
PAIRS = 152
STEPS = [16 * a + 4 * b + c for a in (-1, 0, 1) for b in (-1, 0, 1) for c in (-1, 0, 1)]
OWN = [(x, y, z) for x in (1, 2) for y in (1, 2) for z in (1, 2)]
GHOST = [
    (x, y, z)
    for x in range(4)
    for y in range(4)
    for z in range(4)
    if not (x in (1, 2) and y in (1, 2) and z in (1, 2))
]


def device_at(step, sizes):
    return tuple(
        lax.rem(lax.axis_index(axis) + (move + size), size) if move else lax.axis_index(axis)
        for axis, move, size in zip(AXES, step, sizes)
    )


def leaving(step):
    return tuple({0: pl.ds(1, 2), 1: pl.ds(2, 1), -1: pl.ds(1, 1)}[move] for move in step)


def arriving(step):
    return tuple({0: pl.ds(1, 2), 1: pl.ds(0, 1), -1: pl.ds(3, 1)}[move] for move in step)


def send_all(cells, sizes, send_sem, recv_sem):
    copies = {}
    for index, step in enumerate(AROUND):
        copies[step] = pltpu.make_async_remote_copy(
            src_ref=cells.at[leaving(step)],
            dst_ref=cells.at[arriving(step)],
            send_sem=send_sem.at[index],
            recv_sem=recv_sem.at[index],
            device_id=device_at(step, sizes),
            device_id_type=MESH,
        )
        copies[step].start()
    return copies


def flat(x, y, z):
    return 16 * x + 4 * y + z


def wide(row):
    return jnp.broadcast_to(row, (8, LANES))


def strength(h4):
    h2 = h4 * h4
    q = h2 * h2
    return (2.5 * KERNEL_NORM * 1024.0) / (q * q)


def ranks_of(active):
    live = active == 1
    ahead = lax.broadcasted_iota(jnp.int32, (LANES, LANES), 0) < lax.broadcasted_iota(
        jnp.int32, (LANES, LANES), 1
    )
    before = jnp.dot(
        jnp.where(live, 1.0, 0.0).astype(jnp.bfloat16),
        jnp.where(ahead, 1.0, 0.0).astype(jnp.bfloat16),
        preferred_element_type=F32,
    )
    return jnp.where(live, before, -100.0)


def chosen(ranks, c, group):
    places = lax.broadcasted_iota(jnp.int32, (8, LANES), 0) + 8 * group
    return wide(ranks[pl.ds(c, 1), :]) == places.astype(F32)


def across(tile):
    return jnp.broadcast_to(jnp.sum(tile, axis=1, keepdims=True), (8, LANES))


def density_sum(owns, spread, sites, accs, keep):
    accs = list(accs)
    for index, site in enumerate(sites):
        j = J_TILES * site
        xj, yj, zj, mj = (spread[j + k] for k in (JX, JY, JZ, JM))
        for k, (x, y, z, h4) in enumerate(owns):
            dx = x - xj
            dy = y - yj
            dz = z - zj
            sq = dx * dx + dy * dy + dz * dz
            r4 = sq * lax.rsqrt(jnp.maximum(sq, 1e-30))
            keep(index, k, r4)
            u = jnp.maximum(h4 - r4, 0.0)
            u2 = u * u
            accs[k] = accs[k] + (u2 * u2) * ((0.25 * h4 + r4) * mj)
    return accs


def closing_speed(own, other, sq):
    x, y, z, _, vx, vy, vz, e4 = own[:8]
    xj, yj, zj, uj, vj, wj, ej = other
    app = (x - xj) * (vx - uj) + (y - yj) * (vy - vj) + (z - zj) * (vz - wj)
    e = e4 + ej
    return e * jnp.minimum(app, 0.0) / (sq + e * e)


def motion_of(spread, site):
    return [spread[J_TILES * site + k] for k in (JX, JY, JZ, JU, JV, JW, JE)]


def force_sum(own, spread, states, pairs, acc):
    x, y, z, h4, _, _, _, _, b, rho, fac, sound = own
    ax, ay, az = acc
    for site, r4, m in pairs:
        j = J_TILES * site
        s = S_TILES * site
        dx = x - spread[j + JX]
        dy = y - spread[j + JY]
        dz = z - spread[j + JZ]
        if r4 is None:
            sq = dx * dx + dy * dy + dz * dz
            r4 = sq * lax.rsqrt(jnp.maximum(sq, 1e-30))
        if m is None:
            m = closing_speed(own, motion_of(spread, site), r4 * r4)
        near = jnp.maximum(h4 - r4, 0.0)
        far = jnp.maximum(spread[j + JH] - r4, 0.0)
        visc = m * (m - (sound + states[s + JS])) / (rho + states[s + JR])
        g_near = (near * near) * (near * (b * spread[j + JM]))
        g_far = (far * far) * (far * spread[j + JB])
        w = (fac + visc) * g_near + (states[s + JF] + visc) * g_far
        ax = ax + w * dx
        ay = ay + w * dy
        az = az + w * dz
    return ax, ay, az


def own_values(columns, particles, c, group):
    at = I_TILES * (GROUPS * c + group)
    x, y, z, h4 = (particles[at + k] for k in (IX, IY, IZ, IH))
    column = columns[c, pl.ds(8 * group, 8), :]
    u, v, w, b, entropy = (
        jnp.broadcast_to(column[:, k : k + 1], (8, LANES))
        for k in (FIELDS.index(f) for f in (IU, IV, IW, IB, IF))
    )
    rho = particles[at + IR] * (0.1 * b)
    fac = entropy * jnp.exp(jnp.log(rho) * (-1.0 / 3.0))
    sound = jnp.sqrt((5.0 / 3.0) * fac * rho)
    return [x, y, z, h4, u, v, w, 0.05 * h4, b, rho, 8.0 * fac, sound]


def ghost_sites(c, which):
    gx, gy, gz = 3 * (c // 4), 3 * ((c // 2) % 2), 3 * (c % 2)
    z_side = [flat(x, y, gz) for x in (1, 2) for y in (1, 2)]
    x_side = [flat(gx, y, z) for y in (1, 2) for z in (1, 2, gz)]
    y_side = [flat(x, gy, z) for x in (1, 2) for z in (1, 2, gz)]
    w_side = [flat(gx, gy, z) for z in (1, 2, gz)]
    return {"z": z_side, "x": x_side, "y": y_side, "w": w_side}[which]


def stage_of(step):
    if step[1]:
        return "w" if step[0] else "y"
    return "x" if step[0] else "z"


def outside(place):
    return tuple(0 if k in (1, 2) else 1 for k in place)


def own_sites():
    return [flat(x, y, z) for x, y, z in OWN]


def place_tiles(cells, spread, x, y, z):
    at = J_TILES * flat(x, y, z)
    spread[at + JX] = wide(4.0 * (cells[x, y, z, 0:1, :] + float(x)))
    spread[at + JY] = wide(4.0 * (cells[x, y, z, 1:2, :] + float(y)))
    spread[at + JZ] = wide(4.0 * (cells[x, y, z, 2:3, :] + float(z)))
    spread[at + JM] = wide(cells[x, y, z, 3:4, :])


def motion_tiles(cells, spread, x, y, z):
    at = J_TILES * flat(x, y, z)
    tile = cells[x, y, z]
    h4 = 4.0 * tile[7:8]
    spread[at + JU] = wide(40.0 * tile[4:5])
    spread[at + JV] = wide(40.0 * tile[5:6])
    spread[at + JW] = wide(40.0 * tile[6:7])
    spread[at + JH] = wide(h4)
    spread[at + JE] = wide(0.05 * h4)
    spread[at + JB] = wide(tile[3:4] * strength(h4))


def state_tiles(rho, fac, states, site):
    at = S_TILES * site
    states[at + JR] = wide(rho)
    states[at + JF] = wide(8.0 * fac)
    states[at + JS] = wide(jnp.sqrt((5.0 / 3.0) * fac * rho))


def gather_kernel(
    sizes,
    offsets_in,
    velocities_in,
    smoothing_in,
    mass_in,
    entropy_in,
    prior_in,
    active_in,
    spread,
    particles,
    partial,
    gas,
    ranks,
    density,
    roots,
    slopes,
    columns,
    offsets,
    velocities,
    smoothing,
    mass,
    entropy,
    prior,
    active,
    cells,
    own_states,
    sums,
    picked,
    own_roots,
    load_sem,
    send_sem,
    recv_sem,
    send2_sem,
    recv2_sem,
):
    barrier = pltpu.get_barrier_semaphore()
    for step in AROUND:
        pl.semaphore_signal(
            barrier, inc=1, device_id=device_at(step, sizes), device_id_type=MESH
        )
    loads = [
        pltpu.make_async_copy(source, target, load_sem.at[index])
        for index, (source, target) in enumerate(
            (
                (offsets_in, offsets),
                (velocities_in, velocities),
                (smoothing_in, smoothing),
                (mass_in, mass),
                (entropy_in, entropy),
                (prior_in, prior),
                (active_in, active),
            )
        )
    ]
    for load in loads:
        load.start()
    for load in loads:
        load.wait()

    for c, (x, y, z) in enumerate(OWN):
        rows = [offsets[8 * d + c : 8 * d + c + 1] for d in range(3)]
        rows += [mass[c : c + 1]]
        rows += [velocities[8 * d + c : 8 * d + c + 1] for d in range(3)]
        rows += [smoothing[c : c + 1]]
        for row, value in enumerate(rows):
            cells[x, y, z, row : row + 1, :] = value
    ranks[...] = ranks_of(active[...])

    def spread_columns(c, targets):
        for target in targets:
            source = FIELDS.index(target)
            for group in range(GROUPS):
                particles[I_TILES * (GROUPS * c + group) + target] = jnp.broadcast_to(
                    columns[c, 8 * group : 8 * group + 8, source : source + 1], (8, LANES)
                )

    for c, (x, y, z) in enumerate(OWN):
        tile = cells[x, y, z]
        h4 = 4.0 * tile[7:8]
        picked[0:1, :] = 4.0 * (tile[0:1] + float(x))
        picked[1:2, :] = 4.0 * (tile[1:2] + float(y))
        picked[2:3, :] = 4.0 * (tile[2:3] + float(z))
        picked[3:4, :] = h4
        picked[4:7, :] = 40.0 * tile[4:7]
        picked[7:8, :] = strength(h4)
        picked[8:9, :] = entropy[c : c + 1]
        picked[9:16, :] = jnp.zeros((7, LANES), F32)
        places = lax.broadcasted_iota(jnp.int32, (LANES, LANES), 0).astype(F32)
        found = places == jnp.broadcast_to(ranks[c : c + 1], (LANES, LANES))
        columns[c] = lax.dot_general(
            jnp.where(found, 1.0, 0.0),
            picked[...],
            (((1,), (1,)), ((), ())),
            precision=lax.Precision.HIGHEST,
            preferred_element_type=F32,
        )
        spread_columns(c, (IX, IY, IZ, IH))

    pl.semaphore_wait(barrier, COUNT)
    copies = send_all(cells, sizes, send_sem, recv_sem)
    for x, y, z in OWN:
        place_tiles(cells, spread, x, y, z)

    def density_inputs(t):
        at = I_TILES * t
        return [particles[at + k] for k in (IX, IY, IZ, IH)]

    zero = jnp.zeros((8, LANES), F32)

    def density_part(c, half, sites, first, target, fresh):
        some = [GROUPS * c + 8 * half + k for k in range(8)]

        def keep(index, k, value):
            target[first + index, pl.ds(64 * half + 8 * k, 8), :] = value

        accs = density_sum(
            [density_inputs(t) for t in some],
            spread,
            sites,
            [zero] * 8 if fresh else [sums[t] for t in some],
            keep,
        )
        for t, acc in zip(some, accs):
            sums[t] = acc

    def inner_density(part, carry):
        c = part // 2
        density_part(c, part % 2, own_sites(), 8 * c, own_roots, True)
        return carry

    lax.fori_loop(0, GROUPS, inner_density, 0)

    for which, (base, per_cell) in STAGES.items():
        for step in AROUND:
            if stage_of(step) == which:
                copies[step].wait_recv()
        for x, y, z in GHOST:
            if stage_of(outside((x, y, z))) == which:
                place_tiles(cells, spread, x, y, z)
        if which == "w":
            break
        for c in range(8):

            def outer_density(half, carry, c=c, which=which, first=base + per_cell * c):
                density_part(c, half, ghost_sites(c, which), first, roots, False)
                return carry

            lax.fori_loop(0, 2, outer_density, 0)

    def settle(c):
        total = zero
        for group in range(GROUPS):
            t = GROUPS * c + group
            whole = across(sums[t])
            particles[I_TILES * t + IR] = whole
            total = total + jnp.where(chosen(ranks, c, group), whole, 0.0)
        density[c : c + 1, :] = jnp.sum(total, axis=0, keepdims=True)

    base, per_cell = STAGES["w"]
    for c in range(8):
        for half in range(2):
            density_part(c, half, ghost_sites(c, "w"), base + per_cell * c, roots, False)
        if c:
            settle(c - 1)
    settle(7)
    computed = density[...] * (0.1 * strength(4.0 * smoothing[...]))
    rho = jnp.where(active[...] == 1, computed, prior[...])
    density[...] = rho
    fac = entropy[...] * jnp.exp(jnp.log(rho) * (-1.0 / 3.0))
    for c, (x, y, z) in enumerate(OWN):
        gas[x, y, z, 0:1, :] = rho[c : c + 1]
        gas[x, y, z, 1:2, :] = fac[c : c + 1]
    copies2 = send_all(gas, sizes, send2_sem, recv2_sem)

    for c in range(8):
        for group in range(READY):
            at = I_TILES * (GROUPS * c + group)
            for k, value in enumerate(own_values(columns, particles, c, group)):
                if k > IH:
                    particles[at + k] = value

    for c, (x, y, z) in enumerate(OWN):
        state_tiles(rho[c : c + 1], fac[c : c + 1], own_states, flat(x, y, z))

    for x, y, z in OWN:
        motion_tiles(cells, spread, x, y, z)

    def inner_force(t, carry):
        c, group = t // READY, t % READY
        at = I_TILES * (GROUPS * c + group)
        rows = pl.ds(pl.multiple_of(8 * group, 8), 8)
        acc = force_sum(
            [particles[at + k] for k in range(I_TILES)],
            spread,
            own_states,
            [(site, own_roots[8 * c + k, rows, :], None) for k, site in enumerate(own_sites())],
            (zero, zero, zero),
        )
        for d in range(3):
            partial[3 * t + d] = acc[d]
        return carry

    lax.fori_loop(0, 8 * READY, inner_force, 0)
    for x, y, z in GHOST:
        motion_tiles(cells, spread, x, y, z)
    for c in range(8):
        pairs = [
            (site, base + per_cell * c + k)
            for which, (base, per_cell) in STAGES.items()
            for k, site in enumerate(ghost_sites(c, which))
        ]

        def slope(two, carry, c=c, pairs=pairs):
            owns = [
                [particles[I_TILES * (GROUPS * c + 2 * two + k) + f] for f in range(8)]
                for k in range(2)
            ]
            for site, pair in pairs:
                other = motion_of(spread, site)
                for k, own in enumerate(owns):
                    rows = pl.ds(pl.multiple_of(16 * two, 16) + 8 * k, 8)
                    r4 = roots[pair, rows, :]
                    slopes[pair, rows, :] = closing_speed(own, other, r4 * r4)
            return carry

        lax.fori_loop(0, READY // 2, slope, 0)
    for step in AROUND:
        copies[step].wait_send()
        copies2[step].wait()


def force_kernel(
    spread,
    particles,
    partial,
    gas,
    ranks,
    density_in,
    roots,
    slopes,
    columns,
    density,
    accel,
    states,
    sums,
    counts,
):
    density[...] = density_in[...]
    last = jnp.max(ranks[...], axis=1, keepdims=True)
    for c in range(8):
        counts[c] = (jnp.maximum(jnp.max(last[c : c + 1]), -1.0) + 8.0).astype(jnp.int32) // 8

    def prepare(site, carry):
        state_tiles(gas[site, 0:1, :], gas[site, 1:2, :], states, site)
        return carry

    lax.fori_loop(0, 64, prepare, 0, unroll=4)

    zero = jnp.zeros((8, LANES), F32)
    nothing = (zero, zero, zero)

    def late_cell(c, carry):
        here = flat(1 + c // 4, 1 + (c // 2) % 2, 1 + c % 2)

        def late_group(group, found):
            acc = force_sum(
                own_values(columns, particles, c, group),
                spread,
                states,
                [(here + step, None, None) for step in STEPS],
                nothing,
            )
            mask = chosen(ranks, c, group)
            return tuple(
                total + jnp.where(mask, across(part), 0.0) for total, part in zip(found, acc)
            )

        found = lax.fori_loop(READY, jnp.maximum(counts[c], READY), late_group, nothing)
        for d in range(3):
            accel[pl.ds(8 * d + c, 1), :] = jnp.sum(found[d], axis=0, keepdims=True)
        return carry

    accel[...] = jnp.zeros(accel.shape, F32)

    @pl.when(jnp.max(last) >= 8.0 * READY)
    def late():
        lax.fori_loop(0, 8, late_cell, 0)

    for c in range(8):
        for d in range(3):
            sums[3 * READY * c + d] = zero

    def fold(c, group, totals):
        mask = chosen(ranks, c, group)
        at = 3 * (READY * c + jnp.maximum(group, 0))
        return tuple(
            total + jnp.where(mask, across(sums[at + d]), 0.0) for d, total in enumerate(totals)
        )

    totals = []
    for c in range(8):
        pairs = [
            (site, base + per_cell * c + k)
            for which, (base, per_cell) in STAGES.items()
            for k, site in enumerate(ghost_sites(c, which))
        ]

        def group_step(group, found, c=c, pairs=pairs):
            found = fold(c, group - 1, found)
            at = I_TILES * (GROUPS * c + group)
            t = READY * c + group
            rows = pl.ds(pl.multiple_of(8 * group, 8), 8)
            acc = force_sum(
                [particles[at + k] for k in range(I_TILES)],
                spread,
                states,
                [(site, roots[pair, rows, :], slopes[pair, rows, :]) for site, pair in pairs],
                tuple(partial[3 * t + d] for d in range(3)),
            )
            for d in range(3):
                sums[3 * t + d] = acc[d]
            return found

        totals.append(lax.fori_loop(0, jnp.minimum(counts[c], READY), group_step, nothing))
    for c in range(8):
        found = fold(c, jnp.minimum(counts[c], READY) - 1, totals[c])
        for d in range(3):
            row = slice(8 * d + c, 8 * d + c + 1)
            accel[row, :] = 0.25 * (accel[row, :] + jnp.sum(found[d], axis=0, keepdims=True))


def vmem(count):
    return [pl.BlockSpec(memory_space=pltpu.VMEM)] * count


def tiles(count):
    return jax.ShapeDtypeStruct((count, 8, LANES), F32)


def body(sizes, *args):
    rows = [pltpu.with_memory_space_constraint(a.reshape(-1, LANES), pltpu.HBM) for a in args]
    cell_rows = jax.ShapeDtypeStruct((8, LANES), F32)
    spread, particles, partial, gas, ranks, density, roots, slopes, columns = pl.pallas_call(
        functools.partial(gather_kernel, sizes),
        out_shape=(
            tiles(64 * J_TILES),
            tiles(8 * GROUPS * I_TILES),
            tiles(8 * READY * 3),
            jax.ShapeDtypeStruct((4, 4, 4, 2, LANES), F32),
            cell_rows,
            cell_rows,
            jax.ShapeDtypeStruct((PAIRS, LANES, LANES), F32),
            jax.ShapeDtypeStruct((PAIRS, 8 * READY, LANES), F32),
            jax.ShapeDtypeStruct((8, LANES, 16), F32),
        ),
        in_specs=[pl.BlockSpec(memory_space=pltpu.HBM)] * 7,
        out_specs=tuple(vmem(9)),
        scratch_shapes=[
            pltpu.VMEM((24, LANES), F32),
            pltpu.VMEM((24, LANES), F32),
            pltpu.VMEM((8, LANES), F32),
            pltpu.VMEM((8, LANES), F32),
            pltpu.VMEM((8, LANES), F32),
            pltpu.VMEM((8, LANES), F32),
            pltpu.VMEM((8, LANES), jnp.int32),
            pltpu.VMEM((4, 4, 4, 8, LANES), F32),
            pltpu.VMEM((64 * S_TILES, 8, LANES), F32),
            pltpu.VMEM((8 * GROUPS, 8, LANES), F32),
            pltpu.VMEM((16, LANES), F32),
            pltpu.VMEM((64, LANES, LANES), F32),
            pltpu.SemaphoreType.DMA((7,)),
            pltpu.SemaphoreType.DMA((COUNT,)),
            pltpu.SemaphoreType.DMA((COUNT,)),
            pltpu.SemaphoreType.DMA((COUNT,)),
            pltpu.SemaphoreType.DMA((COUNT,)),
        ],
        compiler_params=pltpu.CompilerParams(
            collective_id=0, has_side_effects=True, vmem_limit_bytes=VMEM_BYTES
        ),
    )(*rows)
    density, accel = pl.pallas_call(
        force_kernel,
        out_shape=(cell_rows, jax.ShapeDtypeStruct((24, LANES), F32)),
        in_specs=vmem(9),
        out_specs=tuple(vmem(2)),
        scratch_shapes=[
            pltpu.VMEM((64 * S_TILES, 8, LANES), F32),
            pltpu.VMEM((8 * READY * 3, 8, LANES), F32),
            pltpu.SMEM((8,), jnp.int32),
        ],
        compiler_params=pltpu.CompilerParams(vmem_limit_bytes=VMEM_BYTES),
    )(spread, particles, partial, gas.reshape(64, 2, LANES), ranks, density, roots, slopes, columns)
    return density.reshape(2, 2, 2, LANES), accel.reshape(3, 2, 2, 2, LANES)


def solution(mesh):
    sizes = tuple(mesh.shape[axis] for axis in AXES)
    spec = P("gx", "gy", "gz", None)
    spec3 = P(None, "gx", "gy", "gz", None)
    return jax.shard_map(
        functools.partial(body, sizes),
        mesh=mesh,
        in_specs=(spec3, spec3, spec, spec, spec, spec, spec),
        out_specs=(spec, spec3),
        check_vma=False,
    )
```
